256 devices in a mesh: seq: 16 (over z, core), clip: 16 (over y, x).
Axes of the slice: x: 4, y: 4, z: 8, core: 2. Of those that a mesh axis runs over, the one named last changes fastest.
Arguments:
- qkv: bfloat16 [16, 2048, 4224], P('clip', 'seq'), may hold values from -6 to 6
- w_out: bfloat16 [1408, 1408], replicated, may hold values from -0.15625 to 0.15625
- enc_gain: float32 [1408], replicated, may hold values from 0.5 to 1.5
- w_embed: bfloat16 [1408, 384], replicated, may hold values from -0.15625 to 0.15625
- pred_gain: float32 [384], replicated, may hold values from 0.5 to 1.5
- ctx_blocks: int32 [192, 12], replicated, may hold values from 0 to 15, as said below
- owner: int32 [192], replicated, may hold values from 0 to 15, as said below
- cotangent: bfloat16 [16, 16, 16, 128, 384], P('clip', 'seq'), may hold values from -6 to 6
Outputs:
- prediction: bfloat16 [16, 16, 16, 128, 384], P('clip', 'seq')
- qkv_grad: bfloat16 [16, 2048, 4224], P('clip', 'seq')
The draws below stay inside these ranges and needn't reach their ends.
Inputs may be any that keep to these rules, and one draw needn't show every extreme that they name: `ctx_blocks`: the 12 blocks of one mask are distinct. `owner`: the 12 masks of one clip have distinct owners.
All inputs are finite; a program needn't handle non-finite values.
Results may differ from the reference program's by a relative error of at most 0.025.
Values may be sent and summed in bfloat16 or wider, within the bound.
A program may use at most 128 MiB of HBM per device.

```python
import jax
import jax.numpy as jnp
from jax import lax

H = 16
E = 88
P_SIZE = 384
BLOCK = 128
D = 1408
SEQ_LEN = 2048
SHARDS = 16
CLIPS = 16
MASKS_CLIP = 12
MASKS = 192
CTX = 12


def draw_qkv(key, part):
    key = jax.random.fold_in(key, 11)
    shape = (CLIPS, SEQ_LEN, H, 3, E)
    values = jnp.clip(jax.random.normal(key, shape, jnp.float32), -6.0, 6.0)
    return values.reshape(CLIPS, SEQ_LEN, H * 3 * E).astype(jnp.bfloat16)


def draw_ctx_blocks(key, part):
    key = jax.random.fold_in(key, 23)
    subkeys = jax.random.split(key, MASKS)
    orders = jax.vmap(lambda single: jax.random.permutation(single, SHARDS))(subkeys)
    return orders[:, :CTX].astype(jnp.int32)


def draw_owner(key, part):
    key = jax.random.fold_in(key, 37)
    subkeys = jax.random.split(key, CLIPS)
    orders = jax.vmap(lambda single: jax.random.permutation(single, CLIPS))(subkeys)
    return orders[:, :MASKS_CLIP].reshape(CLIPS * MASKS_CLIP).astype(jnp.int32)


def block_scale(rng, dims, pieces, smallest, largest):
    loudness = 1.0
    for dim, shards_of in pieces:
        draws = jax.random.uniform(jax.random.fold_in(jax.random.fold_in(rng, 6), dim), (shards_of,), jnp.float32, smallest / len(pieces), largest / len(pieces))
        loudness = loudness * jnp.repeat(jnp.exp(draws), dims[dim] // shards_of).reshape((-1,) + (1,) * (len(dims) - 1 - dim))
    return loudness


def scatter_about(stream_key, shape, scale, limit, cuts=(), held_as=jnp.bfloat16):
    values = jax.random.normal(stream_key, shape, jnp.float32) * scale
    if len(cuts) > 0:
        values = block_scale(stream_key, shape, cuts, -0.22, 0.18) * values
    return jnp.clip(values, min=-limit, max=limit).astype(held_as)


def setup_inputs(seed: int = 0) -> dict:
    splits = jax.random.split(jax.random.key(seed), 9)
    qkv = draw_qkv(jax.random.fold_in(splits[8], 71), 0)
    w_out = scatter_about(splits[1], (D, D), D ** -0.5, 0.15625)
    enc_gain = jnp.clip(1.0 + 0.1 * jax.random.normal(splits[2], (D,), jnp.float32), 0.5, 1.5)
    w_embed = scatter_about(splits[3], (D, P_SIZE), D ** -0.5, 0.15625)
    pred_gain = jnp.clip(1.0 + 0.1 * jax.random.normal(splits[4], (P_SIZE,), jnp.float32), 0.5, 1.5)
    ctx_blocks = draw_ctx_blocks(jax.random.fold_in(splits[8], 71), 0)
    owner = draw_owner(jax.random.fold_in(splits[8], 71), 0)
    cotangent = scatter_about(splits[7], (CLIPS, SHARDS, CLIPS, BLOCK, P_SIZE), 1.0, 6.0, ((0, 16), (1, 16)))
    return {"qkv": qkv, "w_out": w_out, "enc_gain": enc_gain, "w_embed": w_embed, "pred_gain": pred_gain, "ctx_blocks": ctx_blocks, "owner": owner, "cotangent": cotangent}


epsilon = 1e-06

def norm_forward(values, scaling_gain):
    average = lax.optimization_barrier(jnp.mean(values, axis=-1, keepdims=True))
    centred = values - average
    variance = lax.optimization_barrier(jnp.mean(centred * centred, axis=-1, keepdims=True))
    inverse = lax.rsqrt(variance + epsilon)
    normed = centred * inverse
    return (normed * scaling_gain, normed, inverse)

def norm_backward(normed, inverse, upstream):
    average_one = lax.optimization_barrier(jnp.mean(upstream, axis=-1, keepdims=True))
    average_two = lax.optimization_barrier(jnp.mean(upstream * normed, axis=-1, keepdims=True))
    return inverse * (upstream - average_one - normed * average_two)

def mask_table(ctx_blocks, owner, clip_count, shard_count):
    mask_count = owner.shape[0]
    clip_of = jnp.arange(mask_count, dtype=jnp.int32) // (mask_count // clip_count)
    member = jnp.any(ctx_blocks[:, :, None] == jnp.arange(shard_count, dtype=jnp.int32)[None, None, :], axis=1)
    in_clip = clip_of[:, None] == jnp.arange(clip_count, dtype=jnp.int32)[None, :]
    owned_by = owner[:, None] == jnp.arange(clip_count, dtype=jnp.int32)[None, :]
    return jnp.einsum('mc,ms,mo->cso', in_clip.astype(jnp.float32), member.astype(jnp.float32), owned_by.astype(jnp.float32))

def softmax_weights(query_rows, key_rows):
    scaling = query_rows.shape[-1] ** (-0.5)
    scores = jnp.dot(query_rows, key_rows.T, preferred_element_type=jnp.float32) * scaling
    shifted = jnp.exp(scores - lax.optimization_barrier(jnp.max(scores, axis=-1, keepdims=True)))
    return shifted / lax.optimization_barrier(jnp.sum(shifted, axis=-1, keepdims=True))

def head_forward(head_items):
    weights = softmax_weights(head_items[0], head_items[1]).astype(jnp.bfloat16)
    return jnp.dot(weights, head_items[2], preferred_element_type=jnp.float32).astype(jnp.bfloat16)

def head_backward(head_items):
    per_head, output_rows, grad_out = head_items
    query_rows, key_rows, value_rows = (per_head[0], per_head[1], per_head[2])
    scaling = query_rows.shape[-1] ** (-0.5)
    weights = softmax_weights(query_rows, key_rows)
    weights_low = weights.astype(jnp.bfloat16)
    grad_value = jnp.dot(weights_low.T, grad_out, preferred_element_type=jnp.float32)
    grad_weights = jnp.dot(grad_out, value_rows.T, preferred_element_type=jnp.float32)
    correction = lax.optimization_barrier(jnp.sum(grad_out.astype(jnp.float32) * output_rows.astype(jnp.float32), axis=-1, keepdims=True))
    grad_scores = (weights * (grad_weights - correction) * scaling).astype(jnp.bfloat16)
    grad_query = jnp.dot(grad_scores, key_rows, preferred_element_type=jnp.float32)
    grad_key = jnp.dot(grad_scores.T, query_rows, preferred_element_type=jnp.float32)
    return jnp.stack([grad_query, grad_key, grad_value]).astype(jnp.bfloat16)

def encode(clip_qkv, w_out, enc_gain, w_embed, pred_gain):
    per_head = jnp.transpose(clip_qkv.reshape(SEQ_LEN, H, 3, E), (1, 2, 0, 3))
    heads_out = lax.map(head_forward, per_head)
    heads_out = jnp.transpose(heads_out, (1, 0, 2)).reshape(SEQ_LEN, H * E)
    encoded = jnp.dot(heads_out, w_out, preferred_element_type=jnp.float32)
    context, normed_enc, inverse_enc = norm_forward(encoded, enc_gain)
    context = context.astype(jnp.bfloat16)
    embedded = jnp.dot(context, w_embed, preferred_element_type=jnp.float32)
    predicted, normed_emb, inverse_emb = norm_forward(embedded, pred_gain)
    return (per_head, heads_out, predicted.astype(jnp.bfloat16), normed_enc, inverse_enc, normed_emb, inverse_emb)

def reference(qkv, w_out, enc_gain, w_embed, pred_gain, ctx_blocks, owner, cotangent):
    routing = mask_table(ctx_blocks, owner, CLIPS, SHARDS)

    def forward_clip(clip_qkv):
        return encode(clip_qkv, w_out, enc_gain, w_embed, pred_gain)[2]
    predicted = lax.map(forward_clip, qkv).reshape(CLIPS, SHARDS, BLOCK, P_SIZE)
    arranged = jnp.transpose(predicted, (1, 0, 2, 3))[None]
    chosen = jnp.transpose(routing, (2, 1, 0))[:, :, :, None, None] > 0.5
    prediction = jnp.where(chosen, arranged, 0)

    def backward_clip(clip_index):
        clip_qkv = lax.dynamic_index_in_dim(qkv, clip_index, axis=0, keepdims=False)
        per_head, heads_out, unused, normed_enc, inverse_enc, normed_emb, inverse_emb = encode(clip_qkv, w_out, enc_gain, w_embed, pred_gain)
        slot_rows = lax.dynamic_index_in_dim(cotangent, clip_index, axis=2, keepdims=False)
        clip_flags = lax.dynamic_index_in_dim(routing, clip_index, axis=0, keepdims=False)
        grad_predicted = jnp.einsum('so,osbp->sbp', clip_flags, slot_rows.astype(jnp.float32), precision=lax.Precision.HIGHEST).reshape(SEQ_LEN, P_SIZE)
        grad_embedded = norm_backward(normed_emb, inverse_emb, grad_predicted * pred_gain).astype(jnp.bfloat16)
        grad_context = jnp.dot(grad_embedded, w_embed.T, preferred_element_type=jnp.float32)
        grad_encoded = norm_backward(normed_enc, inverse_enc, grad_context * enc_gain).astype(jnp.bfloat16)
        grad_heads = jnp.dot(grad_encoded, w_out.T, preferred_element_type=jnp.float32).astype(jnp.bfloat16)
        grad_split = jnp.transpose(grad_heads.reshape(SEQ_LEN, H, E), (1, 0, 2))
        output_split = jnp.transpose(heads_out.reshape(SEQ_LEN, H, E), (1, 0, 2))
        gradients = lax.map(head_backward, (per_head, output_split, grad_split))
        return jnp.transpose(gradients, (2, 0, 1, 3)).reshape(SEQ_LEN, H * 3 * E)
    qkv_grad = lax.map(backward_clip, jnp.arange(CLIPS, dtype=jnp.int32))
    return (prediction, qkv_grad)
```

```python
import functools

import jax
import jax.numpy as jnp
from jax import lax
from jax.experimental import pallas as pl
from jax.experimental.pallas import tpu as pltpu
from jax.sharding import PartitionSpec as P

E = 88
EP = 96
L = 128
epsilon = 1e-06
MESH = pl.DeviceIdType.MESH
bf16, f32 = jnp.bfloat16, jnp.float32
contract_last = (((1,), (1,)), ((), ()))

KV, Q, HEADS, GRADS, DKV, DQ = range(6)
COT, PRED = range(2)


def dot(a, b):
    return jnp.dot(a, b, preferred_element_type=f32)


def dot_last(a, b):
    return lax.dot_general(a, b, contract_last, preferred_element_type=f32)


def block(index, size=L):
    return pl.ds(pl.multiple_of(index * size, size), size)


def normalize(values):
    average = jnp.mean(values, axis=-1, keepdims=True)
    centred = values - average
    variance = jnp.mean(centred * centred, axis=-1, keepdims=True)
    inverse = lax.rsqrt(variance + epsilon)
    return centred * inverse, inverse


def norm_backward(normed, inverse, upstream):
    average_one = jnp.mean(upstream, axis=-1, keepdims=True)
    average_two = jnp.mean(upstream * normed, axis=-1, keepdims=True)
    return inverse * (upstream - average_one - normed * average_two)


def rows_to(values, rows):
    return jnp.concatenate([values, jnp.zeros((rows - values.shape[0], values.shape[1]), values.dtype)])


def kernel(
    ns,
    nc,
    qkv,
    w_out_hbm,
    enc_gain,
    w_embed,
    pred_gain,
    ctx_blocks,
    owner,
    cot_hbm,
    prediction,
    qkv_grad,
    xt,
    w_out,
    kv_send,
    q_send,
    kvt,
    qt,
    kn,
    vn,
    qn,
    pt,
    ot,
    heads_recv,
    heads_rows,
    cot_recv,
    pred_send,
    pred_recv,
    grads_send,
    dot_t,
    dot_n,
    dq,
    dkv_send,
    dq_send,
    dkv_recv,
    dq_recv,
    seq_send_sem,
    seq_recv_sem,
    clip_send_sem,
    clip_recv_sem,
    local_sem,
):
    me = lax.axis_index("seq")
    clip = lax.axis_index("clip")
    pairs = ns // 2
    my_pair = lax.div(me, 2)
    partner = me + 1 - 2 * lax.rem(me, 2)
    d = ns * E
    tiles = d // L
    scaling = E**-0.5
    to_exp2 = scaling * 1.4426950408889634

    def seq_copy(phase, src, dst, peer):
        return pltpu.make_async_remote_copy(
            src_ref=src,
            dst_ref=dst,
            send_sem=seq_send_sem.at[phase, peer],
            recv_sem=seq_recv_sem.at[phase, me],
            device_id={"seq": peer},
            device_id_type=MESH,
        )

    def seq_wait(phase, dst, source):
        pltpu.make_async_remote_copy(
            src_ref=dst,
            dst_ref=dst,
            send_sem=seq_send_sem.at[phase, source],
            recv_sem=seq_recv_sem.at[phase, source],
            device_id={"seq": source},
            device_id_type=MESH,
        ).wait_recv()

    def clip_copy(phase, src, dst, peer):
        return pltpu.make_async_remote_copy(
            src_ref=src,
            dst_ref=dst,
            send_sem=clip_send_sem.at[phase, peer],
            recv_sem=clip_recv_sem.at[phase, clip],
            device_id={"clip": peer},
            device_id_type=MESH,
        )

    def clip_wait(phase, dst, source):
        pltpu.make_async_remote_copy(
            src_ref=dst,
            dst_ref=dst,
            send_sem=clip_send_sem.at[phase, source],
            recv_sem=clip_recv_sem.at[phase, source],
            device_id={"clip": source},
            device_id_type=MESH,
        ).wait_recv()

    def seq_at(offset):
        return lax.rem(me + offset + ns, ns)

    def clip_at(offset):
        return lax.rem(clip + offset + nc, nc)

    def each(first, last, body):
        def step(i, carry):
            body(i)
            return carry

        lax.fori_loop(first, last, step, 0)

    barrier = pltpu.get_barrier_semaphore()
    each(1, ns, lambda j: pl.semaphore_signal(barrier, inc=1, device_id={"seq": seq_at(j)}, device_id_type=MESH))
    each(1, nc, lambda j: pl.semaphore_signal(barrier, inc=1, device_id={"clip": clip_at(j)}, device_id_type=MESH))

    w_out_copy = pltpu.make_async_copy(w_out_hbm, w_out, local_sem.at[0])
    w_out_copy.start()
    own_cot = pltpu.make_async_copy(cot_hbm.at[0, 0, clip], cot_recv.at[clip], local_sem.at[1])
    own_cot.start()

    for j in range(3 * tiles):
        xt[j * L : (j + 1) * L, :] = qkv[0, :, j * L : (j + 1) * L].astype(f32).T

    def cut(h):
        first = 3 * E * h
        kv_send[h] = xt[pl.ds(pl.multiple_of(first + E, 8), 2 * E), :].astype(bf16)
        q_send[h] = xt[pl.ds(pl.multiple_of(first, 8), EP), :].astype(bf16)

    each(0, ns, cut)
    pl.semaphore_wait(barrier, ns + nc - 2)

    def send_kv(j):
        peer = seq_at(j)
        seq_copy(KV, kv_send.at[peer], kvt.at[:, block(me)], peer).start()

    def send_q(j):
        peer = seq_at(j)
        seq_copy(Q, q_send.at[peer], qt.at[pl.ds(0, EP), block(me)], peer).start()

    def send_cot(j):
        peer = clip_at(j)
        clip_copy(COT, cot_hbm.at[0, 0, peer], cot_recv.at[clip], peer).start()

    each(1, ns, send_kv)
    each(1, ns, send_q)
    each(1, nc, send_cot)

    kvt[:, block(me)] = kv_send[me]
    qt[pl.ds(0, EP), block(me)] = q_send[me]
    qt[pl.ds(EP, L - EP), :] = jnp.zeros((L - EP, ns * L), bf16)
    dot_t[pl.ds(EP, L - EP), :] = jnp.zeros((L - EP, ns * L), bf16)
    dq[...] = jnp.zeros_like(dq)
    masks = owner.shape[1]
    per_clip = masks // nc
    owned = (lax.broadcasted_iota(jnp.int32, (nc, masks), 0) == owner[...]).astype(f32)
    member = jnp.max((ctx_blocks[...] == me).astype(f32), axis=1, keepdims=True)
    mask_id = lax.broadcasted_iota(jnp.int32, (masks, nc), 0)
    first_mask = lax.broadcasted_iota(jnp.int32, (masks, nc), 1) * per_clip
    in_clip = jnp.where((mask_id >= first_mask) & (mask_id < first_mask + per_clip), 1.0, 0.0)
    table = dot(owned, member * in_clip)
    sending = jnp.sum(
        jnp.where(lax.broadcasted_iota(jnp.int32, (nc, nc), 1) == clip, table, 0.0), axis=1, keepdims=True
    )
    receiving = jnp.sum(
        jnp.where(lax.broadcasted_iota(jnp.int32, (nc, nc), 0) == clip, table, 0.0), axis=0, keepdims=True
    )

    def turn_kv(source):
        both = kvt[:, block(source)].astype(f32)
        kn[block(source), :] = rows_to(both[:E], L).T.astype(bf16)
        vn[block(source), :] = rows_to(both[E:], L).T.astype(bf16)

    turn_kv(me)

    def take_kv(j):
        source = seq_at(-j)
        seq_wait(KV, kvt.at[:, block(source)], source)
        turn_kv(source)

    each(1, ns, take_kv)

    def turn_q(source):
        qn[block(source), :] = qt[:, block(source)].astype(f32).T.astype(bf16)

    def attend(pair):
        columns = block(pair, 2 * L)
        scores = dot(kn[...], qt[:, columns])
        shifted = jnp.exp2((scores - jnp.max(scores, axis=0, keepdims=True)) * to_exp2)
        probs = (shifted * (1.0 / jnp.sum(shifted, axis=0, keepdims=True))).astype(bf16)
        pt[:, columns] = probs
        mixed = dot(kvt[2 * E - EP :, :], probs)[EP - E :]
        ot[:, columns] = rows_to(mixed, EP).astype(bf16)

    def wait_q(source):
        seq_wait(Q, qt.at[pl.ds(0, EP), block(source)], source)

    def send_heads(peer):
        seq_copy(HEADS, ot.at[:, block(peer)], heads_recv.at[me], peer).start()

    wait_q(partner)
    attend(my_pair)
    send_heads(partner)
    heads_recv[me] = ot[:, block(me)]
    turn_q(me)
    turn_q(partner)

    def attend_far(i):
        pair = lax.rem(my_pair - i + pairs, pairs)
        wait_q(2 * pair)
        wait_q(2 * pair + 1)
        attend(pair)
        send_heads(2 * pair)
        send_heads(2 * pair + 1)
        turn_q(2 * pair)
        turn_q(2 * pair + 1)

    each(1, pairs, attend_far)

    own_cot.wait()
    each(1, nc, lambda j: clip_wait(COT, cot_recv.at[clip_at(-j)], clip_at(-j)))
    grad_predicted = jnp.zeros((L, cot_recv.shape[2]), f32)
    for o in range(nc):
        grad_predicted += sending[o : o + 1, :] * cot_recv[o].astype(f32)
    w_out_copy.wait()

    def take_heads(j):
        source = seq_at(-j)
        seq_wait(HEADS, heads_recv.at[source], source)

    each(1, ns, take_heads)
    for h in range(ns):
        xt[h * E : (h + 1) * E, :] = heads_recv[h].astype(f32)[:E]
    for j in range(tiles):
        heads_rows[:, j * L : (j + 1) * L] = xt[j * L : (j + 1) * L, :].T.astype(bf16)
    encoded = dot(heads_rows[...], w_out[...])
    normed_enc, inverse_enc = normalize(encoded)
    context = (normed_enc * enc_gain[...]).astype(bf16)
    embedded = dot(context, w_embed[...])
    normed_emb, inverse_emb = normalize(embedded)
    predicted = (normed_emb * pred_gain[...]).astype(bf16)
    pred_send[...] = predicted

    def send_pred(j):
        peer = clip_at(j)
        clip_copy(PRED, pred_send, pred_recv.at[clip], peer).start()

    grad_embedded = norm_backward(normed_emb, inverse_emb, grad_predicted * pred_gain[...]).astype(bf16)
    grad_context = dot_last(grad_embedded, w_embed[...])
    grad_encoded = norm_backward(normed_enc, inverse_enc, grad_context * enc_gain[...]).astype(bf16)
    xt[0:d, :] = dot_last(w_out[...], grad_encoded)

    def cut_grads(j):
        peer = seq_at(j)
        grads_send[peer] = xt[pl.ds(pl.multiple_of(peer * E, 8), EP), :].astype(bf16)
        seq_copy(GRADS, grads_send.at[peer], dot_t.at[pl.ds(0, EP), block(me)], peer).start()

    each(1, ns, cut_grads)
    each(1, nc, send_pred)
    dot_t[pl.ds(0, EP), block(me)] = xt[pl.ds(pl.multiple_of(me * E, 8), EP), :].astype(bf16)
    pred_recv[clip] = predicted

    def turn_grads(source):
        dot_n[block(source), :] = dot_t[:, block(source)].astype(f32).T.astype(bf16)

    turn_grads(me)

    def take_grads(j):
        source = seq_at(-j)
        seq_wait(GRADS, dot_t.at[pl.ds(0, EP), block(source)], source)
        turn_grads(source)

    each(1, ns, take_grads)

    correction = jnp.sum(dot_t[0:EP, :].astype(f32) * ot[...].astype(f32), axis=0, keepdims=True)

    def backward(pair):
        rows = block(pair, 2 * L)
        probs = pt[rows, :]
        grad_probs = dot(vn[rows, :], dot_t[...])
        grad_scores = (probs.astype(f32) * (grad_probs - correction)).astype(bf16)
        grad_value = dot(probs, dot_n[...])
        grad_key = dot(grad_scores, qn[...]) * scaling
        dq[...] += dot(kvt[0:EP, rows], grad_scores)
        dkv_send[:, rows] = jnp.concatenate([grad_key.T[:E], grad_value.T[:E]]).astype(bf16)

    def send_dkv(peer):
        seq_copy(DKV, dkv_send.at[:, block(peer)], dkv_recv.at[me], peer).start()

    def backward_far(i):
        pair = lax.rem(my_pair + i, pairs)
        backward(pair)
        send_dkv(2 * pair)
        send_dkv(2 * pair + 1)

    each(1, pairs, backward_far)
    backward(my_pair)
    send_dkv(partner)
    dkv_recv[me] = dkv_send[:, block(me)]
    dq_send[...] = (dq[...] * scaling).astype(bf16)

    def send_dq(j):
        peer = seq_at(j)
        seq_copy(DQ, dq_send.at[:, block(peer)], dq_recv.at[me], peer).start()

    each(1, ns, send_dq)
    dq_recv[me] = dq_send[:, block(me)]

    each(1, nc, lambda j: clip_wait(PRED, pred_recv.at[clip_at(-j)], clip_at(-j)))
    for c in range(nc):
        prediction[0, 0, c] = (pred_recv[c].astype(f32) * receiving[:, c : c + 1]).astype(bf16)

    def take_grad(j):
        source = seq_at(-j)
        seq_wait(DKV, dkv_recv.at[source], source)
        seq_wait(DQ, dq_recv.at[source], source)

    each(1, ns, take_grad)

    def place(h):
        first = 3 * E * h
        xt[pl.ds(pl.multiple_of(first, 8), E), :] = dq_recv[h].astype(f32)[:E]
        xt[pl.ds(pl.multiple_of(first + E, 8), 2 * E), :] = dkv_recv[h].astype(f32)

    each(0, ns, place)
    for j in range(3 * tiles):
        qkv_grad[0, :, j * L : (j + 1) * L] = xt[j * L : (j + 1) * L, :].T.astype(bf16)

    def sent(j):
        peer = seq_at(j)
        seq_copy(KV, kv_send.at[peer], kvt.at[:, block(me)], peer).wait_send()
        seq_copy(Q, q_send.at[peer], qt.at[pl.ds(0, EP), block(me)], peer).wait_send()
        seq_copy(HEADS, ot.at[:, block(peer)], heads_recv.at[me], peer).wait_send()
        seq_copy(GRADS, grads_send.at[peer], dot_t.at[pl.ds(0, EP), block(me)], peer).wait_send()
        seq_copy(DKV, dkv_send.at[:, block(peer)], dkv_recv.at[me], peer).wait_send()
        seq_copy(DQ, dq_send.at[:, block(peer)], dq_recv.at[me], peer).wait_send()

    def sent_clip(j):
        peer = clip_at(j)
        clip_copy(COT, cot_hbm.at[0, 0, peer], cot_recv.at[clip], peer).wait_send()
        clip_copy(PRED, pred_send, pred_recv.at[clip], peer).wait_send()

    each(1, ns, sent)
    each(1, nc, sent_clip)


def on_device(ns, nc, qkv, w_out, enc_gain, w_embed, pred_gain, ctx_blocks, owner, cotangent):
    d, width = w_embed.shape
    tokens = ns * L
    vmem = pl.BlockSpec(memory_space=pltpu.VMEM)
    hbm = pl.BlockSpec(memory_space=pl.ANY)
    scratch = [
        pltpu.VMEM((3 * d + 16, L), f32),
        pltpu.VMEM((d, d), bf16),
        pltpu.VMEM((ns, 2 * E, L), bf16),
        pltpu.VMEM((ns, EP, L), bf16),
        pltpu.VMEM((2 * E, tokens), bf16),
        pltpu.VMEM((L, tokens), bf16),
        pltpu.VMEM((tokens, L), bf16),
        pltpu.VMEM((tokens, L), bf16),
        pltpu.VMEM((tokens, L), bf16),
        pltpu.VMEM((tokens, tokens), bf16),
        pltpu.VMEM((EP, tokens), bf16),
        pltpu.VMEM((ns, EP, L), bf16),
        pltpu.VMEM((L, d), bf16),
        pltpu.VMEM((nc, L, width), bf16),
        pltpu.VMEM((L, width), bf16),
        pltpu.VMEM((nc, L, width), bf16),
        pltpu.VMEM((ns, EP, L), bf16),
        pltpu.VMEM((L, tokens), bf16),
        pltpu.VMEM((tokens, L), bf16),
        pltpu.VMEM((EP, tokens), f32),
        pltpu.VMEM((2 * E, tokens), bf16),
        pltpu.VMEM((EP, tokens), bf16),
        pltpu.VMEM((ns, 2 * E, L), bf16),
        pltpu.VMEM((ns, EP, L), bf16),
        pltpu.SemaphoreType.DMA((6, ns)),
        pltpu.SemaphoreType.DMA((6, ns)),
        pltpu.SemaphoreType.DMA((2, nc)),
        pltpu.SemaphoreType.DMA((2, nc)),
        pltpu.SemaphoreType.DMA((2,)),
    ]
    prediction, qkv_grad = pl.pallas_call(
        functools.partial(kernel, ns, nc),
        out_shape=(
            jax.ShapeDtypeStruct((1, 1, nc, L, width), bf16),
            jax.ShapeDtypeStruct((1, L, 3 * d), bf16),
        ),
        in_specs=[vmem, hbm, vmem, vmem, vmem, vmem, vmem, hbm],
        out_specs=(vmem, vmem),
        scratch_shapes=scratch,
        compiler_params=pltpu.CompilerParams(
            collective_id=0, has_side_effects=True, vmem_limit_bytes=56 * 1024 * 1024
        ),
        cost_estimate=pl.CostEstimate(flops=16_000_000_000, bytes_accessed=12_000_000, transcendentals=4_194_304),
    )(qkv, w_out, enc_gain[None], w_embed, pred_gain[None], ctx_blocks, owner[None], cotangent)
    return (prediction, qkv_grad)


def solution(mesh):
    placed = (
        P("clip", "seq", None),
        P(),
        P(),
        P(),
        P(),
        P(),
        P(),
        P("clip", "seq", None, None, None),
    )
    return jax.shard_map(
        functools.partial(on_device, mesh.shape["seq"], mesh.shape["clip"]),
        mesh=mesh,
        in_specs=placed,
        out_specs=(P("clip", "seq", None, None, None), P("clip", "seq", None)),
        check_vma=False,
    )
```

```python
import functools

import jax
import jax.numpy as jnp
from jax import lax
from jax.experimental import pallas as pl
from jax.experimental.pallas import tpu as pltpu
from jax.sharding import PartitionSpec as P

E = 88
EP = 96
L = 128
epsilon = 1e-06
MESH = pl.DeviceIdType.MESH
bf16, f32 = jnp.bfloat16, jnp.float32
contract_last = (((1,), (1,)), ((), ()))

KV, Q, HEADS, GRADS, DKV, DQ = range(6)
COT, PRED = range(2)


def dot(a, b):
    return jnp.dot(a, b, preferred_element_type=f32)


def dot_last(a, b):
    return lax.dot_general(a, b, contract_last, preferred_element_type=f32)


def block(index, size=L):
    return pl.ds(pl.multiple_of(index * size, size), size)


def normalize(values):
    average = jnp.mean(values, axis=-1, keepdims=True)
    centred = values - average
    variance = jnp.mean(centred * centred, axis=-1, keepdims=True)
    inverse = lax.rsqrt(variance + epsilon)
    return centred * inverse, inverse


def norm_backward(normed, inverse, upstream):
    average_one = jnp.mean(upstream, axis=-1, keepdims=True)
    average_two = jnp.mean(upstream * normed, axis=-1, keepdims=True)
    return inverse * (upstream - average_one - normed * average_two)


def rows_to(values, rows):
    return jnp.concatenate([values, jnp.zeros((rows - values.shape[0], values.shape[1]), values.dtype)])


def kernel(
    ns,
    nc,
    qkv_hbm,
    w_out_hbm,
    enc_gain,
    w_embed_hbm,
    pred_gain,
    ctx_blocks,
    owner,
    cot_hbm,
    prediction,
    dkv_recv,
    dq_recv,
    xt,
    qkv,
    w_out,
    w_embed,
    kv_send,
    q_send,
    kvt,
    qt,
    kn,
    vn,
    qn,
    pt,
    ot,
    score_rows,
    inverse_total,
    correction,
    heads_recv,
    heads_rows,
    cot_recv,
    pred_send,
    pred_recv,
    grads_send,
    dot_t,
    dot_n,
    dq,
    dkv_send,
    dq_send,
    pred_masked,
    seq_send_sem,
    seq_recv_sem,
    clip_send_sem,
    clip_recv_sem,
    local_sem,
):
    me = lax.axis_index("seq")
    clip = lax.axis_index("clip")
    pairs = ns // 2
    my_pair = lax.div(me, 2)
    partner = me + 1 - 2 * lax.rem(me, 2)
    d = ns * E
    tiles = d // L
    width = w_embed_hbm.shape[1]
    scaling = E**-0.5
    to_exp2 = scaling * 1.4426950408889634

    def seq_copy(phase, src, dst, peer):
        return pltpu.make_async_remote_copy(
            src_ref=src,
            dst_ref=dst,
            send_sem=seq_send_sem.at[phase, peer],
            recv_sem=seq_recv_sem.at[phase, me],
            device_id={"seq": peer},
            device_id_type=MESH,
        )

    def seq_wait(phase, dst, source):
        pltpu.make_async_remote_copy(
            src_ref=dst,
            dst_ref=dst,
            send_sem=seq_send_sem.at[phase, source],
            recv_sem=seq_recv_sem.at[phase, source],
            device_id={"seq": source},
            device_id_type=MESH,
        ).wait_recv()

    def clip_copy(phase, src, dst, peer):
        return pltpu.make_async_remote_copy(
            src_ref=src,
            dst_ref=dst,
            send_sem=clip_send_sem.at[phase, peer],
            recv_sem=clip_recv_sem.at[phase, clip],
            device_id={"clip": peer},
            device_id_type=MESH,
        )

    def clip_wait(phase, dst, source):
        pltpu.make_async_remote_copy(
            src_ref=dst,
            dst_ref=dst,
            send_sem=clip_send_sem.at[phase, source],
            recv_sem=clip_recv_sem.at[phase, source],
            device_id={"clip": source},
            device_id_type=MESH,
        ).wait_recv()

    def seq_at(offset):
        return lax.rem(me + offset + ns, ns)

    def pair_at(i, way=1):
        ahead = (pairs // 2 - lax.div(i, 2)) * (1 - 2 * lax.rem(i, 2))
        return lax.rem(my_pair + way * ahead + 2 * pairs, pairs)

    def each_peer(body, way=1):
        def both(i):
            pair = pair_at(i, way)
            body(2 * pair)
            body(2 * pair + 1)

        body(partner)
        each(1, pairs, both)

    def clip_at(offset):
        return lax.rem(clip + offset + nc, nc)

    def each(first, last, body):
        def step(i, carry):
            body(i)
            return carry

        lax.fori_loop(first, last, step, 0)

    qkv_in = []
    for p in range(3):
        columns = pl.ds(p * d, d)
        qkv_in.append(pltpu.make_async_copy(qkv_hbm.at[0, :, columns], qkv.at[:, columns], local_sem.at[5 + p]))
        qkv_in[-1].start()

    barrier = pltpu.get_barrier_semaphore()
    each(1, ns, lambda j: pl.semaphore_signal(barrier, inc=1, device_id={"seq": seq_at(j)}, device_id_type=MESH))
    each(1, nc, lambda j: pl.semaphore_signal(barrier, inc=1, device_id={"clip": clip_at(j)}, device_id_type=MESH))

    w_out_copy = pltpu.make_async_copy(w_out_hbm, w_out, local_sem.at[0])
    w_out_copy.start()
    w_embed_copy = pltpu.make_async_copy(w_embed_hbm, w_embed, local_sem.at[8])
    w_embed_copy.start()
    own_cot = pltpu.make_async_copy(cot_hbm.at[0, 0, clip], cot_recv.at[clip], local_sem.at[1])
    own_cot.start()

    for p in range(3):
        qkv_in[p].wait()
        for j in range(p * tiles, (p + 1) * tiles):
            xt[j * L : (j + 1) * L, :] = qkv[:, j * L : (j + 1) * L].astype(f32).T
    pl.semaphore_wait(barrier, ns + nc - 2)

    def kv_of(h):
        return xt[pl.ds(pl.multiple_of(3 * E * h + E, 8), 2 * E), :].astype(bf16)

    def q_of(h):
        return xt[pl.ds(pl.multiple_of(3 * E * h, 8), EP), :].astype(bf16)

    def send_kv(peer):
        kv_send[peer] = kv_of(peer)
        seq_copy(KV, kv_send.at[peer], kvt.at[:, block(me)], peer).start()

    def send_q(peer):
        q_send[peer] = q_of(peer)
        seq_copy(Q, q_send.at[peer], qt.at[pl.ds(0, EP), block(me)], peer).start()

    def send_cot(j):
        peer = clip_at(j)
        clip_copy(COT, cot_hbm.at[0, 0, peer], cot_recv.at[clip], peer).start()

    each_peer(send_kv, -1)
    each_peer(send_q, -1)
    each(1, nc, send_cot)

    kvt[:, block(me)] = kv_of(me)
    qt[pl.ds(0, EP), block(me)] = q_of(me)
    qt[pl.ds(EP, L - EP), :] = jnp.zeros((L - EP, ns * L), bf16)
    dot_t[pl.ds(EP, L - EP), :] = jnp.zeros((L - EP, ns * L), bf16)
    dq[...] = jnp.zeros_like(dq)
    masks = owner.shape[1]
    per_clip = masks // nc
    owned = (lax.broadcasted_iota(jnp.int32, (nc, masks), 0) == owner[...]).astype(f32)
    member = jnp.max((ctx_blocks[...] == me).astype(f32), axis=0, keepdims=True)
    mask_id = lax.broadcasted_iota(jnp.int32, (masks, nc), 0)
    first_mask = lax.broadcasted_iota(jnp.int32, (masks, nc), 1) * per_clip
    in_clip = jnp.where((mask_id >= first_mask) & (mask_id < first_mask + per_clip), 1.0, 0.0)
    table = dot(owned * member, in_clip)
    sending = jnp.sum(
        jnp.where(lax.broadcasted_iota(jnp.int32, (nc, nc), 1) == clip, table, 0.0), axis=1, keepdims=True
    )
    receiving = jnp.sum(
        jnp.where(lax.broadcasted_iota(jnp.int32, (nc, nc), 0) == clip, table, 0.0), axis=0, keepdims=True
    )

    def turn_kv(source):
        both = kvt[:, block(source)].astype(f32)
        kn[block(source), :] = rows_to(both[:E], L).T.astype(bf16)
        vn[block(source), :] = rows_to(both[E:], L).T.astype(bf16)

    turn_kv(me)

    def take_kv(j):
        source = seq_at(-j)
        seq_wait(KV, kvt.at[:, block(source)], source)
        turn_kv(source)

    each(1, ns, take_kv)

    def turn_q(source):
        qn[block(source), :] = qt[:, block(source)].astype(f32).T.astype(bf16)

    def attend(pair):
        columns = block(pair, 2 * L)
        queries = qt[:, columns]
        largest = None
        for k in range(pairs):
            keys = slice(2 * L * k, 2 * L * (k + 1))
            scores = dot(kn[keys, :], queries)
            score_rows[keys, :] = scores
            part = jnp.max(scores.reshape(2 * L // 8, 8, 2 * L), axis=0)
            largest = part if largest is None else jnp.maximum(largest, part)
        largest = jnp.max(largest, axis=0, keepdims=True)
        total = jnp.zeros((8, 2 * L), f32)
        mixed = jnp.zeros((EP, 2 * L), f32)
        for k in range(pairs):
            keys = slice(2 * L * k, 2 * L * (k + 1))
            shifted = jnp.exp2((score_rows[keys, :] - largest) * to_exp2)
            total += jnp.sum(shifted.reshape(2 * L // 8, 8, 2 * L), axis=0)
            probs = shifted.astype(bf16)
            pt[keys, columns] = probs
            mixed += dot(kvt[2 * E - EP :, keys], probs)
        inverse = 1.0 / jnp.sum(total, axis=0, keepdims=True)
        inverse_total[:, columns] = inverse
        ot[:, columns] = rows_to(mixed[EP - E :] * inverse, EP).astype(bf16)

    def wait_q(source):
        seq_wait(Q, qt.at[pl.ds(0, EP), block(source)], source)

    def send_heads(peer):
        seq_copy(HEADS, ot.at[:, block(peer)], heads_recv.at[me], peer).start()

    wait_q(partner)
    attend(my_pair)
    send_heads(partner)
    heads_recv[me] = ot[:, block(me)]
    turn_q(me)
    turn_q(partner)

    def attend_far(i):
        pair = pair_at(i)
        wait_q(2 * pair)
        wait_q(2 * pair + 1)
        attend(pair)
        send_heads(2 * pair)
        send_heads(2 * pair + 1)
        turn_q(2 * pair)
        turn_q(2 * pair + 1)

    each(1, pairs, attend_far)

    own_cot.wait()
    each(1, nc, lambda j: clip_wait(COT, cot_recv.at[clip_at(-j)], clip_at(-j)))
    grad_predicted = jnp.zeros((L, cot_recv.shape[2]), f32)
    for o in range(nc):
        grad_predicted += sending[o : o + 1, :] * cot_recv[o].astype(f32)
    w_out_copy.wait()
    w_embed_copy.wait()

    def take_heads(j):
        source = seq_at(-j)
        seq_wait(HEADS, heads_recv.at[source], source)

    each(1, ns, take_heads)
    for h in range(ns):
        xt[h * E : (h + 1) * E, :] = heads_recv[h].astype(f32)[:E]
    for j in range(tiles):
        heads_rows[:, j * L : (j + 1) * L] = xt[j * L : (j + 1) * L, :].T.astype(bf16)
    encoded = dot(heads_rows[...], w_out[...])
    normed_enc, inverse_enc = normalize(encoded)
    context = (normed_enc * enc_gain[...].reshape(1, d)).astype(bf16)
    embedded = dot(context, w_embed[...])
    normed_emb, inverse_emb = normalize(embedded)
    predicted = (normed_emb * pred_gain[...].reshape(1, width)).astype(bf16)
    pred_send[...] = predicted

    def send_pred(j):
        peer = clip_at(j)
        clip_copy(PRED, pred_send, pred_recv.at[clip], peer).start()

    grad_embedded = norm_backward(normed_emb, inverse_emb, grad_predicted * pred_gain[...].reshape(1, width)).astype(bf16)
    grad_context = dot_last(grad_embedded, w_embed[...])
    grad_encoded = norm_backward(normed_enc, inverse_enc, grad_context * enc_gain[...].reshape(1, d)).astype(bf16)
    xt[0:d, :] = dot_last(w_out[...], grad_encoded)

    def cut_grads(peer):
        grads_send[peer] = xt[pl.ds(pl.multiple_of(peer * E, 8), EP), :].astype(bf16)
        seq_copy(GRADS, grads_send.at[peer], dot_t.at[pl.ds(0, EP), block(me)], peer).start()

    each_peer(cut_grads)
    each(1, nc, send_pred)
    dot_t[pl.ds(0, EP), block(me)] = xt[pl.ds(pl.multiple_of(me * E, 8), EP), :].astype(bf16)
    pred_recv[clip] = predicted

    def turn_grads(source):
        rounded = (dot_t[:, block(source)].astype(f32) * inverse_total[:, block(source)]).astype(bf16)
        dot_t[:, block(source)] = rounded
        scaled = rounded.astype(f32)
        dot_n[block(source), :] = scaled.T.astype(bf16)
        mixed = ot[:, block(source)].astype(f32)
        correction[:, block(source)] = jnp.sum(scaled[:EP] * mixed, axis=0, keepdims=True)

    turn_grads(me)

    def take_grads(j):
        source = seq_at(-j)
        seq_wait(GRADS, dot_t.at[pl.ds(0, EP), block(source)], source)
        turn_grads(source)

    each(1, ns, take_grads)

    def backward(pair):
        rows = block(pair, 2 * L)
        probs = pt[rows, :]
        grad_probs = dot(vn[rows, :], dot_t[...])
        grad_scores = (probs.astype(f32) * (grad_probs - correction[...])).astype(bf16)
        grad_value = dot(probs, dot_n[...])
        grad_key = dot(grad_scores, qn[...]) * scaling
        dq[...] += dot(kvt[0:EP, rows], grad_scores)
        dkv_send[:, rows] = jnp.concatenate([grad_key.T[:E], grad_value.T[:E]]).astype(bf16)

    def send_dkv(peer):
        seq_copy(DKV, dkv_send.at[:, block(peer)], dkv_recv.at[me], peer).start()

    def backward_far(i):
        pair = pair_at(i)
        backward(pair)
        send_dkv(2 * pair)
        send_dkv(2 * pair + 1)

    each(1, pairs, backward_far)
    backward(my_pair)
    send_dkv(partner)
    own_dkv = pltpu.make_async_copy(dkv_send.at[:, block(me)], dkv_recv.at[me], local_sem.at[3])
    own_dkv.start()
    dq_send[...] = (dq[...] * scaling).astype(bf16)

    def send_dq(peer):
        seq_copy(DQ, dq_send.at[:, block(peer)], dq_recv.at[me], peer).start()

    each_peer(send_dq)
    own_dq = pltpu.make_async_copy(dq_send.at[:, block(me)], dq_recv.at[me], local_sem.at[4])
    own_dq.start()

    each(1, nc, lambda j: clip_wait(PRED, pred_recv.at[clip_at(-j)], clip_at(-j)))
    for c in range(nc):
        pred_masked[c] = (pred_recv[c].astype(f32) * receiving[:, c : c + 1]).astype(bf16)
    pred_copy = pltpu.make_async_copy(pred_masked, prediction, local_sem.at[2])
    pred_copy.start()

    def take_grad(j):
        source = seq_at(-j)
        seq_wait(DKV, dkv_recv.at[source], source)
        seq_wait(DQ, dq_recv.at[source], source)

    each(1, ns, take_grad)
    own_dkv.wait()
    own_dq.wait()
    pred_copy.wait()

    def sent(j):
        peer = seq_at(j)
        seq_copy(KV, kv_send.at[peer], kvt.at[:, block(me)], peer).wait_send()
        seq_copy(Q, q_send.at[peer], qt.at[pl.ds(0, EP), block(me)], peer).wait_send()
        seq_copy(HEADS, ot.at[:, block(peer)], heads_recv.at[me], peer).wait_send()
        seq_copy(GRADS, grads_send.at[peer], dot_t.at[pl.ds(0, EP), block(me)], peer).wait_send()
        seq_copy(DKV, dkv_send.at[:, block(peer)], dkv_recv.at[me], peer).wait_send()
        seq_copy(DQ, dq_send.at[:, block(peer)], dq_recv.at[me], peer).wait_send()

    def sent_clip(j):
        peer = clip_at(j)
        clip_copy(COT, cot_hbm.at[0, 0, peer], cot_recv.at[clip], peer).wait_send()
        clip_copy(PRED, pred_send, pred_recv.at[clip], peer).wait_send()

    each(1, ns, sent)
    each(1, nc, sent_clip)


def finish(ns, parts, masked_hbm, dkv_hbm, dq_hbm, prediction, qkv_grad, masked, dkv, dq, xt, turned, sems):
    tiles = qkv_grad.shape[2] // L
    thirds = tiles // 3
    each_part = masked.shape[0] // parts
    dkv_in = pltpu.make_async_copy(dkv_hbm, dkv, sems.at[0])
    dq_in = pltpu.make_async_copy(dq_hbm, dq, sems.at[1])
    dkv_in.start()
    dq_in.start()
    blocks_in, blocks_out = [], []
    for p in range(parts):
        some = pl.ds(p * each_part, each_part)
        blocks_in.append(pltpu.make_async_copy(masked_hbm.at[some], masked.at[some], sems.at[2 + p]))
        blocks_out.append(pltpu.make_async_copy(masked.at[some], prediction.at[0, 0, some], sems.at[2 + parts + p]))
    for copy in blocks_in:
        copy.start()
    dkv_in.wait()
    dq_in.wait()
    for h in range(ns):
        first = 3 * E * h
        xt[first : first + E, :] = dq[h].astype(f32)[:E]
        xt[first + E : first + 3 * E, :] = dkv[h].astype(f32)
    grads_out = []
    for p in range(3):
        for j in range(p * thirds, (p + 1) * thirds):
            turned[:, j * L : (j + 1) * L] = xt[j * L : (j + 1) * L, :].T.astype(bf16)
        columns = pl.ds(p * thirds * L, thirds * L)
        grads_out.append(pltpu.make_async_copy(turned.at[:, columns], qkv_grad.at[0, :, columns], sems.at[2 + 2 * parts + p]))
        grads_out[-1].start()
        for q in range(p * parts // 3, (p + 1) * parts // 3):
            blocks_in[q].wait()
            blocks_out[q].start()
    for copy in blocks_out + grads_out:
        copy.wait()


def on_device(ns, nc, qkv, w_out, enc_gain, w_embed, pred_gain, ctx_blocks, owner, cotangent):
    d, width = w_embed.shape
    tokens = ns * L
    vmem = pl.BlockSpec(memory_space=pltpu.VMEM)
    hbm = pl.BlockSpec(memory_space=pl.ANY)
    scratch = [
        pltpu.VMEM((3 * d + 16, L), f32),
        pltpu.VMEM((L, 3 * d), bf16),
        pltpu.VMEM((d, d), bf16),
        pltpu.VMEM((d, width), bf16),
        pltpu.VMEM((ns, 2 * E, L), bf16),
        pltpu.VMEM((ns, EP, L), bf16),
        pltpu.VMEM((2 * E, tokens), bf16),
        pltpu.VMEM((L, tokens), bf16),
        pltpu.VMEM((tokens, L), bf16),
        pltpu.VMEM((tokens, L), bf16),
        pltpu.VMEM((tokens, L), bf16),
        pltpu.VMEM((tokens, tokens), bf16),
        pltpu.VMEM((EP, tokens), bf16),
        pltpu.VMEM((tokens, 2 * L), f32),
        pltpu.VMEM((1, tokens), f32),
        pltpu.VMEM((1, tokens), f32),
        pltpu.VMEM((ns, EP, L), bf16),
        pltpu.VMEM((L, d), bf16),
        pltpu.VMEM((nc, L, width), bf16),
        pltpu.VMEM((L, width), bf16),
        pltpu.VMEM((nc, L, width), bf16),
        pltpu.VMEM((ns, EP, L), bf16),
        pltpu.VMEM((L, tokens), bf16),
        pltpu.VMEM((tokens, L), bf16),
        pltpu.VMEM((EP, tokens), f32),
        pltpu.VMEM((2 * E, tokens), bf16),
        pltpu.VMEM((EP, tokens), bf16),
        pltpu.VMEM((nc, L, width), bf16),
        pltpu.SemaphoreType.DMA((6, ns)),
        pltpu.SemaphoreType.DMA((6, ns)),
        pltpu.SemaphoreType.DMA((2, nc)),
        pltpu.SemaphoreType.DMA((2, nc)),
        pltpu.SemaphoreType.DMA((9,)),
    ]
    prediction, dkv, dq = pl.pallas_call(
        functools.partial(kernel, ns, nc),
        out_shape=(
            jax.ShapeDtypeStruct((nc, L, width), bf16),
            jax.ShapeDtypeStruct((ns, 2 * E, L), bf16),
            jax.ShapeDtypeStruct((ns, EP, L), bf16),
        ),
        in_specs=[hbm, hbm, vmem, hbm, vmem, vmem, vmem, hbm],
        out_specs=(hbm, hbm, hbm),
        scratch_shapes=scratch,
        compiler_params=pltpu.CompilerParams(
            collective_id=0, has_side_effects=True, vmem_limit_bytes=56 * 1024 * 1024
        ),
        cost_estimate=pl.CostEstimate(flops=16_000_000_000, bytes_accessed=12_000_000, transcendentals=4_194_304),
    )(qkv, w_out, enc_gain, w_embed, pred_gain, ctx_blocks.T, owner[None], cotangent)
    parts = min(nc, 4)
    return pl.pallas_call(
        functools.partial(finish, ns, parts),
        out_shape=(
            jax.ShapeDtypeStruct((1, 1, nc, L, width), bf16),
            jax.ShapeDtypeStruct((1, L, 3 * d), bf16),
        ),
        in_specs=[hbm, hbm, hbm],
        out_specs=(hbm, hbm),
        scratch_shapes=[
            pltpu.VMEM((nc, L, width), bf16),
            pltpu.VMEM((ns, 2 * E, L), bf16),
            pltpu.VMEM((ns, EP, L), bf16),
            pltpu.VMEM((3 * d, L), f32),
            pltpu.VMEM((L, 3 * d), bf16),
            pltpu.SemaphoreType.DMA((5 + 2 * parts,)),
        ],
        compiler_params=pltpu.CompilerParams(vmem_limit_bytes=56 * 1024 * 1024),
        cost_estimate=pl.CostEstimate(flops=0, bytes_accessed=6_000_000, transcendentals=0),
    )(prediction, dkv, dq)


def solution(mesh):
    placed = (
        P("clip", "seq", None),
        P(),
        P(),
        P(),
        P(),
        P(),
        P(),
        P("clip", "seq", None, None, None),
    )
    return jax.shard_map(
        functools.partial(on_device, mesh.shape["seq"], mesh.shape["clip"]),
        mesh=mesh,
        in_specs=placed,
        out_specs=(P("clip", "seq", None, None, None), P("clip", "seq", None)),
        check_vma=False,
    )
```

```python
import functools

import jax
import jax.numpy as jnp
from jax import lax
from jax.experimental import pallas as pl
from jax.experimental.pallas import tpu as pltpu
from jax.sharding import PartitionSpec as P

E = 88
EP = 96
L = 128
epsilon = 1e-06
MESH = pl.DeviceIdType.MESH
bf16, f32 = jnp.bfloat16, jnp.float32
contract_last = (((1,), (1,)), ((), ()))

KV, Q, HEADS, GRADS, DKV, DQ = range(6)
COT, PRED = range(2)


def dot(a, b):
    return jnp.dot(a, b, preferred_element_type=f32)


def dot_last(a, b):
    return lax.dot_general(a, b, contract_last, preferred_element_type=f32)


def block(index, size=L):
    return pl.ds(pl.multiple_of(index * size, size), size)


def normalize(values):
    average = jnp.mean(values, axis=-1, keepdims=True)
    centred = values - average
    variance = jnp.mean(centred * centred, axis=-1, keepdims=True)
    inverse = lax.rsqrt(variance + epsilon)
    return centred * inverse, inverse


def norm_backward(normed, inverse, upstream):
    average_one = jnp.mean(upstream, axis=-1, keepdims=True)
    average_two = jnp.mean(upstream * normed, axis=-1, keepdims=True)
    return inverse * (upstream - average_one - normed * average_two)


def rows_to(values, rows):
    return jnp.concatenate([values, jnp.zeros((rows - values.shape[0], values.shape[1]), values.dtype)])


def kernel(
    ns,
    nc,
    qkv_hbm,
    w_out_hbm,
    enc_gain,
    w_embed_hbm,
    pred_gain,
    ctx_blocks,
    owner,
    cot_hbm,
    prediction,
    dkv_recv,
    dq_recv,
    xt,
    qkv,
    w_out,
    w_embed,
    kv_send,
    q_send,
    kvt,
    qt,
    kn,
    vn,
    qn,
    pt,
    ot,
    score_rows,
    inverse_total,
    correction,
    heads_recv,
    heads_rows,
    cot_recv,
    pred_send,
    pred_recv,
    grads_send,
    dot_t,
    dot_n,
    dq,
    dk_sum,
    dv_sum,
    dkv_send,
    dq_send,
    pred_masked,
    seq_send_sem,
    seq_recv_sem,
    clip_send_sem,
    clip_recv_sem,
    local_sem,
):
    me = lax.axis_index("seq")
    clip = lax.axis_index("clip")
    pairs = ns // 2
    my_pair = lax.div(me, 2)
    partner = me + 1 - 2 * lax.rem(me, 2)
    quads = ns // 4
    my_quad = lax.div(me, 4)
    d = ns * E
    tiles = d // L
    width = w_embed_hbm.shape[1]
    scaling = E**-0.5
    to_exp2 = scaling * 1.4426950408889634

    def seq_copy(phase, src, dst, peer):
        return pltpu.make_async_remote_copy(
            src_ref=src,
            dst_ref=dst,
            send_sem=seq_send_sem.at[phase, peer],
            recv_sem=seq_recv_sem.at[phase, me],
            device_id={"seq": peer},
            device_id_type=MESH,
        )

    def seq_wait(phase, dst, source):
        pltpu.make_async_remote_copy(
            src_ref=dst,
            dst_ref=dst,
            send_sem=seq_send_sem.at[phase, source],
            recv_sem=seq_recv_sem.at[phase, source],
            device_id={"seq": source},
            device_id_type=MESH,
        ).wait_recv()

    def clip_copy(phase, src, dst, peer):
        return pltpu.make_async_remote_copy(
            src_ref=src,
            dst_ref=dst,
            send_sem=clip_send_sem.at[phase, peer],
            recv_sem=clip_recv_sem.at[phase, clip],
            device_id={"clip": peer},
            device_id_type=MESH,
        )

    def clip_wait(phase, dst, source):
        pltpu.make_async_remote_copy(
            src_ref=dst,
            dst_ref=dst,
            send_sem=clip_send_sem.at[phase, source],
            recv_sem=clip_recv_sem.at[phase, source],
            device_id={"clip": source},
            device_id_type=MESH,
        ).wait_recv()

    def seq_at(offset):
        return lax.rem(me + offset + ns, ns)

    def pair_at(i, way=1):
        ahead = (pairs // 2 - lax.div(i, 2)) * (1 - 2 * lax.rem(i, 2))
        return lax.rem(my_pair + way * ahead + 2 * pairs, pairs)

    def place_of(source):
        return block(lax.rem(source, 2) * pairs + lax.div(source, 2))

    def quad_at(i):
        ahead = jnp.where(i == 0, 0, (quads // 2 - lax.div(i, 2)) * (1 - 2 * lax.rem(i, 2)))
        return lax.rem(my_quad + ahead + 2 * quads, quads)

    def members(core, quad):
        return 4 * quad + core, 4 * quad + 2 + core

    def unless_me(source, body):
        pl.when(source != me)(lambda: body(source))

    def each_peer(body, way=1):
        def both(i):
            pair = pair_at(i, way)
            body(2 * pair)
            body(2 * pair + 1)

        body(partner)
        each(1, pairs, both)

    def clip_at(offset):
        return lax.rem(clip + offset + nc, nc)

    def each(first, last, body):
        def step(i, carry):
            body(i)
            return carry

        lax.fori_loop(first, last, step, 0)

    qkv_in = []
    for p in range(3):
        columns = pl.ds(p * d, d)
        qkv_in.append(pltpu.make_async_copy(qkv_hbm.at[0, :, columns], qkv.at[:, columns], local_sem.at[5 + p]))
        qkv_in[-1].start()

    barrier = pltpu.get_barrier_semaphore()
    each(1, ns, lambda j: pl.semaphore_signal(barrier, inc=1, device_id={"seq": seq_at(j)}, device_id_type=MESH))
    each(1, nc, lambda j: pl.semaphore_signal(barrier, inc=1, device_id={"clip": clip_at(j)}, device_id_type=MESH))

    w_out_copy = pltpu.make_async_copy(w_out_hbm, w_out, local_sem.at[0])
    w_out_copy.start()
    w_embed_copy = pltpu.make_async_copy(w_embed_hbm, w_embed, local_sem.at[8])
    w_embed_copy.start()
    own_cot = pltpu.make_async_copy(cot_hbm.at[0, 0, clip], cot_recv.at[clip], local_sem.at[1])
    own_cot.start()

    for p in range(3):
        qkv_in[p].wait()
        for j in range(p * tiles, (p + 1) * tiles):
            xt[j * L : (j + 1) * L, :] = qkv[:, j * L : (j + 1) * L].astype(f32).T
    pl.semaphore_wait(barrier, ns + nc - 2)

    def kv_of(h):
        return xt[pl.ds(pl.multiple_of(3 * E * h + E, 8), 2 * E), :].astype(bf16)

    def q_of(h):
        return xt[pl.ds(pl.multiple_of(3 * E * h, 8), EP), :].astype(bf16)

    def send_kv(peer):
        kv_send[peer] = kv_of(peer)
        seq_copy(KV, kv_send.at[peer], kvt.at[:, place_of(me)], peer).start()

    def send_q(peer):
        q_send[peer] = q_of(peer)
        seq_copy(Q, q_send.at[peer], qt.at[pl.ds(0, EP), place_of(me)], peer).start()

    def send_cot(j):
        peer = clip_at(j)
        clip_copy(COT, cot_hbm.at[0, 0, peer], cot_recv.at[clip], peer).start()

    each_peer(send_kv, -1)
    each_peer(send_q, -1)
    each(1, nc, send_cot)

    kvt[:, place_of(me)] = kv_of(me)
    qt[pl.ds(0, EP), place_of(me)] = q_of(me)
    qt[pl.ds(EP, L - EP), :] = jnp.zeros((L - EP, ns * L), bf16)
    dot_t[pl.ds(EP, L - EP), :] = jnp.zeros((L - EP, ns * L), bf16)
    dq[...] = jnp.zeros_like(dq)
    dk_sum[...] = jnp.zeros_like(dk_sum)
    dv_sum[...] = jnp.zeros_like(dv_sum)
    masks = owner.shape[1]
    per_clip = masks // nc
    owned = (lax.broadcasted_iota(jnp.int32, (nc, masks), 0) == owner[...]).astype(f32)
    member = jnp.max((ctx_blocks[...] == me).astype(f32), axis=0, keepdims=True)
    mask_id = lax.broadcasted_iota(jnp.int32, (masks, nc), 0)
    first_mask = lax.broadcasted_iota(jnp.int32, (masks, nc), 1) * per_clip
    in_clip = jnp.where((mask_id >= first_mask) & (mask_id < first_mask + per_clip), 1.0, 0.0)
    table = dot(owned * member, in_clip)
    sending = jnp.sum(
        jnp.where(lax.broadcasted_iota(jnp.int32, (nc, nc), 1) == clip, table, 0.0), axis=1, keepdims=True
    )
    receiving = jnp.sum(
        jnp.where(lax.broadcasted_iota(jnp.int32, (nc, nc), 0) == clip, table, 0.0), axis=0, keepdims=True
    )

    def turn_kv(source):
        both = kvt[:, place_of(source)].astype(f32)
        kn[place_of(source), :] = rows_to(both[:E], L).T.astype(bf16)
        vn[place_of(source), :] = rows_to(both[E:], L).T.astype(bf16)

    turn_kv(me)

    def take_kv(j):
        source = seq_at(-j)
        seq_wait(KV, kvt.at[:, place_of(source)], source)
        turn_kv(source)

    each(1, ns, take_kv)

    def turn_q(source):
        qn[place_of(source), :] = qt[:, place_of(source)].astype(f32).T.astype(bf16)

    def attend(pair):
        columns = block(pair, 2 * L)
        queries = qt[:, columns]
        largest = None
        for k in range(pairs):
            keys = slice(2 * L * k, 2 * L * (k + 1))
            scores = dot(kn[keys, :], queries)
            score_rows[keys, :] = scores
            part = jnp.max(scores.reshape(2 * L // 8, 8, 2 * L), axis=0)
            largest = part if largest is None else jnp.maximum(largest, part)
        largest = jnp.max(largest, axis=0, keepdims=True)
        total = jnp.zeros((8, 2 * L), f32)
        mixed = jnp.zeros((EP, 2 * L), f32)
        for k in range(pairs):
            keys = slice(2 * L * k, 2 * L * (k + 1))
            shifted = jnp.exp2((score_rows[keys, :] - largest) * to_exp2)
            total += jnp.sum(shifted.reshape(2 * L // 8, 8, 2 * L), axis=0)
            probs = shifted.astype(bf16)
            pt[keys, columns] = probs
            mixed += dot(kvt[2 * E - EP :, keys], probs)
        inverse = 1.0 / jnp.sum(total, axis=0, keepdims=True)
        inverse_total[:, columns] = inverse
        ot[:, columns] = rows_to(mixed[EP - E :] * inverse, EP).astype(bf16)

    def wait_q(source):
        seq_wait(Q, qt.at[pl.ds(0, EP), place_of(source)], source)

    def send_heads(peer):
        seq_copy(HEADS, ot.at[:, place_of(peer)], heads_recv.at[me], peer).start()

    def keep_heads(source):
        heads_recv[me] = ot[:, place_of(me)]

    def attend_core(core):
        def step(i):
            quad = quad_at(i)
            first, second = members(core, quad)
            unless_me(first, wait_q)
            unless_me(second, wait_q)
            attend(core * quads + quad)
            unless_me(first, send_heads)
            unless_me(second, send_heads)
            turn_q(first)
            turn_q(second)

        each(1, quads, step)
        step(0 * me)

    attend_core(0)
    attend_core(1)
    keep_heads(me)

    own_cot.wait()
    each(1, nc, lambda j: clip_wait(COT, cot_recv.at[clip_at(-j)], clip_at(-j)))
    grad_predicted = jnp.zeros((L, cot_recv.shape[2]), f32)
    for o in range(nc):
        grad_predicted += sending[o : o + 1, :] * cot_recv[o].astype(f32)
    w_out_copy.wait()
    w_embed_copy.wait()

    def take_heads(j):
        source = seq_at(-j)
        seq_wait(HEADS, heads_recv.at[source], source)

    each(1, ns, take_heads)
    for h in range(ns):
        xt[h * E : (h + 1) * E, :] = heads_recv[h].astype(f32)[:E]
    for j in range(tiles):
        heads_rows[:, j * L : (j + 1) * L] = xt[j * L : (j + 1) * L, :].T.astype(bf16)
    encoded = dot(heads_rows[...], w_out[...])
    normed_enc, inverse_enc = normalize(encoded)
    context = (normed_enc * enc_gain[...].reshape(1, d)).astype(bf16)
    embedded = dot(context, w_embed[...])
    normed_emb, inverse_emb = normalize(embedded)
    predicted = (normed_emb * pred_gain[...].reshape(1, width)).astype(bf16)
    pred_send[...] = predicted

    def send_pred(j):
        peer = clip_at(j)
        clip_copy(PRED, pred_send, pred_recv.at[clip], peer).start()

    grad_embedded = norm_backward(normed_emb, inverse_emb, grad_predicted * pred_gain[...].reshape(1, width)).astype(bf16)
    grad_context = dot_last(grad_embedded, w_embed[...])
    grad_encoded = norm_backward(normed_enc, inverse_enc, grad_context * enc_gain[...].reshape(1, d)).astype(bf16)
    xt[0:d, :] = dot_last(w_out[...], grad_encoded)

    def cut_grads(peer):
        grads_send[peer] = xt[pl.ds(pl.multiple_of(peer * E, 8), EP), :].astype(bf16)
        seq_copy(GRADS, grads_send.at[peer], dot_t.at[pl.ds(0, EP), place_of(me)], peer).start()

    each_peer(cut_grads)
    each(1, nc, send_pred)
    dot_t[pl.ds(0, EP), place_of(me)] = xt[pl.ds(pl.multiple_of(me * E, 8), EP), :].astype(bf16)
    pred_recv[clip] = predicted

    def turn_grads(source):
        rounded = (dot_t[:, place_of(source)].astype(f32) * inverse_total[:, place_of(source)]).astype(bf16)
        dot_t[:, place_of(source)] = rounded
        scaled = rounded.astype(f32)
        dot_n[place_of(source), :] = scaled.T.astype(bf16)
        mixed = ot[:, place_of(source)].astype(f32)
        correction[:, place_of(source)] = jnp.sum(scaled[:EP] * mixed, axis=0, keepdims=True)

    def take_grads(source):
        def wait():
            seq_wait(GRADS, dot_t.at[pl.ds(0, EP), place_of(source)], source)

        pl.when(source != me)(wait)
        turn_grads(source)

    def send_dkv(peer):
        seq_copy(DKV, dkv_send.at[:, place_of(peer)], dkv_recv.at[me], peer).start()

    def send_dq(peer):
        seq_copy(DQ, dq_send.at[:, place_of(peer)], dq_recv.at[me], peer).start()

    def backward_queries(pair):
        columns = block(pair, 2 * L)
        grads_t, grads_n, queries = dot_t[:, columns], dot_n[columns, :], qn[columns, :]
        shift = correction[:, columns]
        grad_query = jnp.zeros((EP, 2 * L), f32)
        for k in range(pairs):
            keys = slice(2 * L * k, 2 * L * (k + 1))
            probs = pt[keys, columns]
            grad_probs = dot(vn[keys, :], grads_t)
            grad_scores = (probs.astype(f32) * (grad_probs - shift)).astype(bf16)
            grad_query += dot(kvt[0:EP, keys], grad_scores)
            dv_sum[keys, :] += dot(probs, grads_n)
            dk_sum[keys, :] += dot(grad_scores, queries)
        dq_send[:, columns] = (grad_query * scaling).astype(bf16)

    def first_core(i):
        quad = quad_at(i)
        first, second = members(0, quad)
        take_grads(first)
        take_grads(second)
        backward_queries(quad)
        unless_me(first, send_dq)
        unless_me(second, send_dq)

    each(1, quads, first_core)
    first_core(0 * me)

    def take_second(i):
        quad = quad_at(i)
        first, second = members(1, quad)
        take_grads(first)
        take_grads(second)

    each(0, quads, take_second)
    half = pairs * L

    def backward_keys(pair):
        rows = block(pair, 2 * L)
        probs = pt[rows, half:]
        grad_probs = dot(vn[rows, :], dot_t[:, half:])
        grad_scores = (probs.astype(f32) * (grad_probs - correction[:, half:])).astype(bf16)
        grad_value = dv_sum[rows, :] + dot(probs, dot_n[half:, :])
        grad_key = (dk_sum[rows, :] + dot(grad_scores, qn[half:, :])) * scaling
        dq[...] += dot(kvt[0:EP, rows], grad_scores)
        dkv_send[:, rows] = jnp.concatenate([grad_key.T[:E], grad_value.T[:E]]).astype(bf16)

    def second_core(i):
        quad = quad_at(i)
        for core in range(2):
            first, second = members(core, quad)
            backward_keys(core * quads + quad)
            unless_me(first, send_dkv)
            unless_me(second, send_dkv)

    each(1, quads, second_core)
    second_core(0 * me)
    dq_send[:, half:] = (dq[...] * scaling).astype(bf16)

    def send_second(i):
        quad = quad_at(i)
        first, second = members(1, quad)
        unless_me(first, send_dq)
        unless_me(second, send_dq)

    each(1, quads, send_second)
    send_second(0 * me)
    own_dkv = pltpu.make_async_copy(dkv_send.at[:, place_of(me)], dkv_recv.at[me], local_sem.at[3])
    own_dkv.start()
    own_dq = pltpu.make_async_copy(dq_send.at[:, place_of(me)], dq_recv.at[me], local_sem.at[4])
    own_dq.start()

    each(1, nc, lambda j: clip_wait(PRED, pred_recv.at[clip_at(-j)], clip_at(-j)))
    for c in range(nc):
        pred_masked[c] = (pred_recv[c].astype(f32) * receiving[:, c : c + 1]).astype(bf16)
    pred_copy = pltpu.make_async_copy(pred_masked, prediction, local_sem.at[2])
    pred_copy.start()

    def take_grad(j):
        source = seq_at(-j)
        seq_wait(DKV, dkv_recv.at[source], source)
        seq_wait(DQ, dq_recv.at[source], source)

    each(1, ns, take_grad)
    own_dkv.wait()
    own_dq.wait()
    pred_copy.wait()

    def sent(j):
        peer = seq_at(j)
        seq_copy(KV, kv_send.at[peer], kvt.at[:, place_of(me)], peer).wait_send()
        seq_copy(Q, q_send.at[peer], qt.at[pl.ds(0, EP), place_of(me)], peer).wait_send()
        seq_copy(HEADS, ot.at[:, place_of(peer)], heads_recv.at[me], peer).wait_send()
        seq_copy(GRADS, grads_send.at[peer], dot_t.at[pl.ds(0, EP), place_of(me)], peer).wait_send()
        seq_copy(DKV, dkv_send.at[:, place_of(peer)], dkv_recv.at[me], peer).wait_send()
        seq_copy(DQ, dq_send.at[:, place_of(peer)], dq_recv.at[me], peer).wait_send()

    def sent_clip(j):
        peer = clip_at(j)
        clip_copy(COT, cot_hbm.at[0, 0, peer], cot_recv.at[clip], peer).wait_send()
        clip_copy(PRED, pred_send, pred_recv.at[clip], peer).wait_send()

    each(1, ns, sent)
    each(1, nc, sent_clip)


def finish(ns, parts, masked_hbm, dkv_hbm, dq_hbm, prediction, qkv_grad, masked, dkv, dq, xt, turned, sems):
    tiles = qkv_grad.shape[2] // L
    thirds = tiles // 3
    each_part = masked.shape[0] // parts
    dkv_in = pltpu.make_async_copy(dkv_hbm, dkv, sems.at[0])
    dq_in = pltpu.make_async_copy(dq_hbm, dq, sems.at[1])
    dkv_in.start()
    dq_in.start()
    blocks_in, blocks_out = [], []
    for p in range(parts):
        some = pl.ds(p * each_part, each_part)
        blocks_in.append(pltpu.make_async_copy(masked_hbm.at[some], masked.at[some], sems.at[2 + p]))
        blocks_out.append(pltpu.make_async_copy(masked.at[some], prediction.at[0, 0, some], sems.at[2 + parts + p]))
    for copy in blocks_in:
        copy.start()
    dkv_in.wait()
    dq_in.wait()
    for h in range(ns):
        first = 3 * E * h
        xt[first : first + E, :] = dq[h].astype(f32)[:E]
        xt[first + E : first + 3 * E, :] = dkv[h].astype(f32)
    grads_out = []
    for p in range(3):
        for j in range(p * thirds, (p + 1) * thirds):
            turned[:, j * L : (j + 1) * L] = xt[j * L : (j + 1) * L, :].T.astype(bf16)
        columns = pl.ds(p * thirds * L, thirds * L)
        grads_out.append(pltpu.make_async_copy(turned.at[:, columns], qkv_grad.at[0, :, columns], sems.at[2 + 2 * parts + p]))
        grads_out[-1].start()
        for q in range(p * parts // 3, (p + 1) * parts // 3):
            blocks_in[q].wait()
            blocks_out[q].start()
    for copy in blocks_out + grads_out:
        copy.wait()


def on_device(ns, nc, qkv, w_out, enc_gain, w_embed, pred_gain, ctx_blocks, owner, cotangent):
    d, width = w_embed.shape
    tokens = ns * L
    vmem = pl.BlockSpec(memory_space=pltpu.VMEM)
    hbm = pl.BlockSpec(memory_space=pl.ANY)
    scratch = [
        pltpu.VMEM((3 * d + 16, L), f32),
        pltpu.VMEM((L, 3 * d), bf16),
        pltpu.VMEM((d, d), bf16),
        pltpu.VMEM((d, width), bf16),
        pltpu.VMEM((ns, 2 * E, L), bf16),
        pltpu.VMEM((ns, EP, L), bf16),
        pltpu.VMEM((2 * E, tokens), bf16),
        pltpu.VMEM((L, tokens), bf16),
        pltpu.VMEM((tokens, L), bf16),
        pltpu.VMEM((tokens, L), bf16),
        pltpu.VMEM((tokens, L), bf16),
        pltpu.VMEM((tokens, tokens), bf16),
        pltpu.VMEM((EP, tokens), bf16),
        pltpu.VMEM((tokens, 2 * L), f32),
        pltpu.VMEM((1, tokens), f32),
        pltpu.VMEM((1, tokens), f32),
        pltpu.VMEM((ns, EP, L), bf16),
        pltpu.VMEM((L, d), bf16),
        pltpu.VMEM((nc, L, width), bf16),
        pltpu.VMEM((L, width), bf16),
        pltpu.VMEM((nc, L, width), bf16),
        pltpu.VMEM((ns, EP, L), bf16),
        pltpu.VMEM((L, tokens), bf16),
        pltpu.VMEM((tokens, L), bf16),
        pltpu.VMEM((EP, tokens // 2), f32),
        pltpu.VMEM((tokens, L), f32),
        pltpu.VMEM((tokens, L), f32),
        pltpu.VMEM((2 * E, tokens), bf16),
        pltpu.VMEM((EP, tokens), bf16),
        pltpu.VMEM((nc, L, width), bf16),
        pltpu.SemaphoreType.DMA((6, ns)),
        pltpu.SemaphoreType.DMA((6, ns)),
        pltpu.SemaphoreType.DMA((2, nc)),
        pltpu.SemaphoreType.DMA((2, nc)),
        pltpu.SemaphoreType.DMA((9,)),
    ]
    prediction, dkv, dq = pl.pallas_call(
        functools.partial(kernel, ns, nc),
        out_shape=(
            jax.ShapeDtypeStruct((nc, L, width), bf16),
            jax.ShapeDtypeStruct((ns, 2 * E, L), bf16),
            jax.ShapeDtypeStruct((ns, EP, L), bf16),
        ),
        in_specs=[hbm, hbm, vmem, hbm, vmem, vmem, vmem, hbm],
        out_specs=(hbm, hbm, hbm),
        scratch_shapes=scratch,
        compiler_params=pltpu.CompilerParams(
            collective_id=0, has_side_effects=True, vmem_limit_bytes=56 * 1024 * 1024
        ),
        cost_estimate=pl.CostEstimate(flops=16_000_000_000, bytes_accessed=12_000_000, transcendentals=4_194_304),
    )(qkv, w_out, enc_gain, w_embed, pred_gain, ctx_blocks.T, owner[None], cotangent)
    parts = min(nc, 4)
    return pl.pallas_call(
        functools.partial(finish, ns, parts),
        out_shape=(
            jax.ShapeDtypeStruct((1, 1, nc, L, width), bf16),
            jax.ShapeDtypeStruct((1, L, 3 * d), bf16),
        ),
        in_specs=[hbm, hbm, hbm],
        out_specs=(hbm, hbm),
        scratch_shapes=[
            pltpu.VMEM((nc, L, width), bf16),
            pltpu.VMEM((ns, 2 * E, L), bf16),
            pltpu.VMEM((ns, EP, L), bf16),
            pltpu.VMEM((3 * d, L), f32),
            pltpu.VMEM((L, 3 * d), bf16),
            pltpu.SemaphoreType.DMA((5 + 2 * parts,)),
        ],
        compiler_params=pltpu.CompilerParams(vmem_limit_bytes=56 * 1024 * 1024),
        cost_estimate=pl.CostEstimate(flops=0, bytes_accessed=6_000_000, transcendentals=0),
    )(prediction, dkv, dq)


def solution(mesh):
    placed = (
        P("clip", "seq", None),
        P(),
        P(),
        P(),
        P(),
        P(),
        P(),
        P("clip", "seq", None, None, None),
    )
    return jax.shard_map(
        functools.partial(on_device, mesh.shape["seq"], mesh.shape["clip"]),
        mesh=mesh,
        in_specs=placed,
        out_specs=(P("clip", "seq", None, None, None), P("clip", "seq", None)),
        check_vma=False,
    )
```

```python
import functools

import jax
import jax.numpy as jnp
from jax import lax
from jax.experimental import pallas as pl
from jax.experimental.pallas import tpu as pltpu
from jax.sharding import PartitionSpec as P

E = 88
EP = 96
L = 128
epsilon = 1e-06
MESH = pl.DeviceIdType.MESH
bf16, f32 = jnp.bfloat16, jnp.float32
contract_last = (((1,), (1,)), ((), ()))

QK, V, HEADS, GRADS, DKV, DQ = range(6)
COT, PRED = range(2)


def dot(a, b):
    return jnp.dot(a, b, preferred_element_type=f32)


def dot_last(a, b):
    return lax.dot_general(a, b, contract_last, preferred_element_type=f32)


def block(index, size=L):
    return pl.ds(pl.multiple_of(index * size, size), size)


def normalize(values):
    average = jnp.mean(values, axis=-1, keepdims=True)
    centred = values - average
    variance = jnp.mean(centred * centred, axis=-1, keepdims=True)
    inverse = lax.rsqrt(variance + epsilon)
    return centred * inverse, inverse


def norm_backward(normed, inverse, upstream):
    average_one = jnp.mean(upstream, axis=-1, keepdims=True)
    average_two = jnp.mean(upstream * normed, axis=-1, keepdims=True)
    return inverse * (upstream - average_one - normed * average_two)


def rows_to(values, rows):
    return jnp.concatenate([values, jnp.zeros((rows - values.shape[0], values.shape[1]), values.dtype)])


def kernel(
    ns,
    nc,
    qkv_hbm,
    w_out_hbm,
    enc_gain,
    w_embed_hbm,
    pred_gain,
    ctx_blocks,
    owner,
    cot_hbm,
    prediction,
    dkv_recv,
    dq_recv,
    xt,
    qkv,
    w_out,
    w_embed,
    qk_send,
    v_send,
    qkt,
    vt,
    qt,
    kn,
    vn,
    qn,
    pt,
    ot,
    score_rows,
    inverse_total,
    correction,
    heads_recv,
    heads_rows,
    cot_recv,
    pred_send,
    pred_recv,
    grads_send,
    dot_t,
    dot_n,
    dq,
    dk_sum,
    dv_sum,
    dkv_send,
    dq_send,
    pred_masked,
    seq_send_sem,
    seq_recv_sem,
    clip_send_sem,
    clip_recv_sem,
    local_sem,
    ready,
):
    me = lax.axis_index("seq")
    clip = lax.axis_index("clip")
    pairs = ns // 2
    my_pair = lax.div(me, 2)
    partner = me + 1 - 2 * lax.rem(me, 2)
    quads = ns // 4
    my_quad = lax.div(me, 4)
    d = ns * E
    tiles = d // L
    width = w_embed_hbm.shape[1]
    scaling = E**-0.5
    to_exp2 = scaling * 1.4426950408889634

    def seq_copy(phase, src, dst, peer):
        return pltpu.make_async_remote_copy(
            src_ref=src,
            dst_ref=dst,
            send_sem=seq_send_sem.at[phase, peer],
            recv_sem=seq_recv_sem.at[phase, me],
            device_id={"seq": peer},
            device_id_type=MESH,
        )

    def seq_wait(phase, dst, source):
        pltpu.make_async_remote_copy(
            src_ref=dst,
            dst_ref=dst,
            send_sem=seq_send_sem.at[phase, source],
            recv_sem=seq_recv_sem.at[phase, source],
            device_id={"seq": source},
            device_id_type=MESH,
        ).wait_recv()

    def clip_copy(phase, src, dst, peer):
        return pltpu.make_async_remote_copy(
            src_ref=src,
            dst_ref=dst,
            send_sem=clip_send_sem.at[phase, peer],
            recv_sem=clip_recv_sem.at[phase, clip],
            device_id={"clip": peer},
            device_id_type=MESH,
        )

    def clip_wait(phase, dst, source):
        pltpu.make_async_remote_copy(
            src_ref=dst,
            dst_ref=dst,
            send_sem=clip_send_sem.at[phase, source],
            recv_sem=clip_recv_sem.at[phase, source],
            device_id={"clip": source},
            device_id_type=MESH,
        ).wait_recv()

    def seq_at(offset):
        return lax.rem(me + offset + ns, ns)

    def pair_at(i, way=1):
        ahead = (pairs // 2 - lax.div(i, 2)) * (1 - 2 * lax.rem(i, 2))
        return lax.rem(my_pair + way * ahead + 2 * pairs, pairs)

    def place_of(source):
        return block(lax.rem(source, 2) * pairs + lax.div(source, 2))

    def quad_at(i):
        ahead = jnp.where(i == 0, 0, (quads // 2 - lax.div(i, 2)) * (1 - 2 * lax.rem(i, 2)))
        return lax.rem(my_quad + ahead + 2 * quads, quads)

    def members(core, quad):
        return 4 * quad + core, 4 * quad + 2 + core

    def unless_me(source, body):
        pl.when(source != me)(lambda: body(source))

    def each_peer(body, way=1):
        def both(i):
            pair = pair_at(i, way)
            body(2 * pair)
            body(2 * pair + 1)

        body(partner)
        each(1, pairs, both)

    def clip_at(offset):
        return lax.rem(clip + offset + nc, nc)

    def each(first, last, body):
        def step(i, carry):
            body(i)
            return carry

        lax.fori_loop(first, last, step, 0)

    qkv_in = []
    for p in range(3):
        columns = pl.ds(p * d, d)
        qkv_in.append(pltpu.make_async_copy(qkv_hbm.at[0, :, columns], qkv.at[:, columns], local_sem.at[5 + p]))
        qkv_in[-1].start()

    barrier = pltpu.get_barrier_semaphore()
    each(1, ns, lambda j: pl.semaphore_signal(barrier, inc=1, device_id={"seq": seq_at(j)}, device_id_type=MESH))
    each(
        clip + 1,
        nc,
        lambda c: pl.semaphore_signal(barrier, inc=1, device_id={"clip": c}, device_id_type=MESH),
    )

    w_out_copy = pltpu.make_async_copy(w_out_hbm, w_out, local_sem.at[0])
    w_out_copy.start()
    w_embed_copy = pltpu.make_async_copy(w_embed_hbm, w_embed, local_sem.at[8])
    w_embed_copy.start()
    own_cot = pltpu.make_async_copy(cot_hbm.at[0, 0, clip], cot_recv.at[clip], local_sem.at[1])
    own_cot.start()

    for p in range(3):
        qkv_in[p].wait()
        for j in range(p * tiles, (p + 1) * tiles):
            xt[j * L : (j + 1) * L, :] = qkv[:, j * L : (j + 1) * L].astype(f32).T
    pl.semaphore_wait(barrier, ns - 1 + clip)
    each(0, clip, lambda c: pl.semaphore_signal(ready, inc=1, device_id={"clip": c}, device_id_type=MESH))

    xt[pl.ds(3 * d, 16), :] = jnp.zeros((16, L), f32)

    def qk_of(h):
        return xt[pl.ds(pl.multiple_of(3 * E * h, 8), 2 * E), :].astype(bf16)

    def v_of(h):
        return xt[pl.ds(pl.multiple_of(3 * E * h + 2 * E, 8), EP), :].astype(bf16)

    def send_qk(peer):
        qk_send[peer] = qk_of(peer)
        seq_copy(QK, qk_send.at[peer], qkt.at[:, place_of(me)], peer).start()

    def send_v(peer):
        v_send[peer] = v_of(peer)
        seq_copy(V, v_send.at[peer], vt.at[:, place_of(me)], peer).start()

    def send_cot(j):
        peer = clip_at(j)
        clip_copy(COT, cot_hbm.at[0, 0, peer], cot_recv.at[clip], peer).start()

    each_peer(send_qk, -1)
    each_peer(send_v, -1)

    qkt[:, place_of(me)] = qk_of(me)
    vt[:, place_of(me)] = v_of(me)
    dot_t[pl.ds(EP, L - EP), :] = jnp.zeros((L - EP, ns * L), bf16)
    dq[...] = jnp.zeros_like(dq)
    dk_sum[...] = jnp.zeros_like(dk_sum)
    dv_sum[...] = jnp.zeros_like(dv_sum)
    masks = owner.shape[1]
    per_clip = masks // nc
    owned = (lax.broadcasted_iota(jnp.int32, (nc, masks), 0) == owner[...]).astype(f32)
    member = jnp.max((ctx_blocks[...] == me).astype(f32), axis=0, keepdims=True)
    mask_id = lax.broadcasted_iota(jnp.int32, (masks, nc), 0)
    first_mask = lax.broadcasted_iota(jnp.int32, (masks, nc), 1) * per_clip
    in_clip = jnp.where((mask_id >= first_mask) & (mask_id < first_mask + per_clip), 1.0, 0.0)
    table = dot(owned * member, in_clip)
    sending = jnp.sum(
        jnp.where(lax.broadcasted_iota(jnp.int32, (nc, nc), 1) == clip, table, 0.0), axis=1, keepdims=True
    )
    receiving = jnp.sum(
        jnp.where(lax.broadcasted_iota(jnp.int32, (nc, nc), 0) == clip, table, 0.0), axis=0, keepdims=True
    )

    def turn_qk(source):
        both = qkt[:, place_of(source)].astype(f32)
        query, key = rows_to(both[:E], L), rows_to(both[E:], L)
        qt[:, place_of(source)] = query.astype(bf16)
        qn[place_of(source), :] = query.T.astype(bf16)
        kn[place_of(source), :] = key.T.astype(bf16)

    turn_qk(me)

    def take_qk(j):
        source = seq_at(-j)
        seq_wait(QK, qkt.at[:, place_of(source)], source)
        turn_qk(source)

    each(7, 10, take_qk)
    pl.when(clip < nc - 1)(lambda: pl.semaphore_wait(ready, nc - 1 - clip))
    each(1, nc, send_cot)
    each(1, 7, take_qk)
    each(10, ns, take_qk)

    def weigh(pair, carry):
        columns = block(pair, 2 * L)
        queries = qt[:, columns]
        largest = None
        for k in range(pairs):
            keys = slice(2 * L * k, 2 * L * (k + 1))
            scores = dot(kn[keys, :], queries)
            score_rows[keys, :] = scores
            part = jnp.max(scores.reshape(2 * L // 8, 8, 2 * L), axis=0)
            largest = part if largest is None else jnp.maximum(largest, part)
        largest = jnp.max(largest, axis=0, keepdims=True)
        total = jnp.zeros((8, 2 * L), f32)
        for k in range(pairs):
            keys = slice(2 * L * k, 2 * L * (k + 1))
            shifted = jnp.exp2((score_rows[keys, :] - largest) * to_exp2)
            total += jnp.sum(shifted.reshape(2 * L // 8, 8, 2 * L), axis=0)
            pt[keys, columns] = shifted.astype(bf16)
        inverse_total[:, columns] = 1.0 / jnp.sum(total, axis=0, keepdims=True)
        return carry

    lax.fori_loop(0, pairs, weigh, 0)

    def wait_v(source):
        seq_wait(V, vt.at[:, place_of(source)], source)

    def turn_v(source):
        vn[place_of(source), :] = rows_to(vt[:, place_of(source)].astype(f32)[:E], L).T.astype(bf16)

    def send_heads(peer):
        seq_copy(HEADS, ot.at[:, place_of(peer)], heads_recv.at[me], peer).start()

    def mix_core(core):
        def step(i):
            quad = quad_at(i)
            first, second = members(core, quad)
            columns = block(core * quads + quad, 2 * L)
            mixed = dot(vt[...], pt[:, columns])[:E] * inverse_total[:, columns]
            ot[:, columns] = rows_to(mixed, EP).astype(bf16)
            unless_me(first, send_heads)
            unless_me(second, send_heads)

        each(1, quads, step)
        step(0 * me)


    def heads_sent(peer):
        seq_copy(HEADS, ot.at[:, place_of(peer)], heads_recv.at[me], peer).wait_send()

    def sent_core(first_i, last_i, core):
        def step(i):
            first, second = members(core, quad_at(i))
            unless_me(first, heads_sent)
            unless_me(second, heads_sent)

        each(first_i, last_i, step)

    each(1, ns, lambda j: wait_v(seq_at(-j)))
    mix_core(0)
    each(0, ns, turn_v)
    sent_core(1, 1 + 3, 0)
    mix_core(1)
    heads_recv[me] = ot[:, place_of(me)]

    own_cot.wait()
    each(1, nc, lambda j: clip_wait(COT, cot_recv.at[clip_at(-j)], clip_at(-j)))
    grad_predicted = jnp.zeros((L, cot_recv.shape[2]), f32)
    for o in range(nc):
        grad_predicted += sending[o : o + 1, :] * cot_recv[o].astype(f32)
    w_out_copy.wait()
    w_embed_copy.wait()

    def take_heads(j):
        source = seq_at(-j)
        seq_wait(HEADS, heads_recv.at[source], source)

    each(1, ns, take_heads)
    for h in range(ns):
        xt[h * E : (h + 1) * E, :] = heads_recv[h].astype(f32)[:E]
    for j in range(tiles):
        heads_rows[:, j * L : (j + 1) * L] = xt[j * L : (j + 1) * L, :].T.astype(bf16)
    encoded = dot(heads_rows[...], w_out[...])
    normed_enc, inverse_enc = normalize(encoded)
    context = (normed_enc * enc_gain[...].reshape(1, d)).astype(bf16)
    embedded = dot(context, w_embed[...])
    normed_emb, inverse_emb = normalize(embedded)
    predicted = (normed_emb * pred_gain[...].reshape(1, width)).astype(bf16)
    pred_send[...] = predicted

    def send_pred(j):
        peer = clip_at(j)
        clip_copy(PRED, pred_send, pred_recv.at[clip], peer).start()

    grad_embedded = norm_backward(normed_emb, inverse_emb, grad_predicted * pred_gain[...].reshape(1, width)).astype(bf16)
    grad_context = dot_last(grad_embedded, w_embed[...])
    grad_encoded = norm_backward(normed_enc, inverse_enc, grad_context * enc_gain[...].reshape(1, d)).astype(bf16)
    xt[0:d, :] = dot_last(w_out[...], grad_encoded)

    def cut_grads(peer):
        grads_send[peer] = xt[pl.ds(pl.multiple_of(peer * E, 8), EP), :].astype(bf16)
        seq_copy(GRADS, grads_send.at[peer], dot_t.at[pl.ds(0, EP), place_of(me)], peer).start()

    each_peer(cut_grads)
    each(1, nc, send_pred)
    dot_t[pl.ds(0, EP), place_of(me)] = xt[pl.ds(pl.multiple_of(me * E, 8), EP), :].astype(bf16)
    pred_recv[clip] = predicted

    def turn_grads(source):
        rounded = (dot_t[:, place_of(source)].astype(f32) * inverse_total[:, place_of(source)]).astype(bf16)
        dot_t[:, place_of(source)] = rounded
        scaled = rounded.astype(f32)
        dot_n[place_of(source), :] = scaled.T.astype(bf16)
        mixed = ot[:, place_of(source)].astype(f32)
        correction[:, place_of(source)] = jnp.sum(scaled[:EP] * mixed, axis=0, keepdims=True)

    def take_grads(source):
        def wait():
            seq_wait(GRADS, dot_t.at[pl.ds(0, EP), place_of(source)], source)

        pl.when(source != me)(wait)
        turn_grads(source)

    def send_dkv(peer):
        seq_copy(DKV, dkv_send.at[:, place_of(peer)], dkv_recv.at[me], peer).start()

    def send_dq(peer):
        seq_copy(DQ, dq_send.at[:, place_of(peer)], dq_recv.at[me], peer).start()

    def backward_queries(pair):
        columns = block(pair, 2 * L)
        grads_t, grads_n, queries = dot_t[:, columns], dot_n[columns, :], qn[columns, :]
        shift = correction[:, columns]
        grad_query = jnp.zeros((EP, 2 * L), f32)
        for k in range(pairs):
            keys = slice(2 * L * k, 2 * L * (k + 1))
            probs = pt[keys, columns]
            grad_probs = dot(vn[keys, :], grads_t)
            grad_scores = (probs.astype(f32) * (grad_probs - shift)).astype(bf16)
            grad_query += dot(qkt[2 * E - EP :, keys], grad_scores)
            dv_sum[keys, :] += dot(probs, grads_n)
            dk_sum[keys, :] += dot(grad_scores, queries)
        dq_send[:, columns] = rows_to(grad_query[EP - E :] * scaling, EP).astype(bf16)

    def first_core(i):
        quad = quad_at(i)
        first, second = members(0, quad)
        take_grads(first)
        take_grads(second)
        backward_queries(quad)
        unless_me(first, send_dq)
        unless_me(second, send_dq)

    each(1, quads, first_core)
    first_core(0 * me)

    def take_second(i):
        quad = quad_at(i)
        first, second = members(1, quad)
        take_grads(first)
        take_grads(second)

    each(0, quads, take_second)
    half = pairs * L

    def backward_keys(pair):
        rows = block(pair, 2 * L)
        probs = pt[rows, half:]
        grad_probs = dot(vn[rows, :], dot_t[:, half:])
        grad_scores = (probs.astype(f32) * (grad_probs - correction[:, half:])).astype(bf16)
        grad_value = dv_sum[rows, :] + dot(probs, dot_n[half:, :])
        grad_key = (dk_sum[rows, :] + dot(grad_scores, qn[half:, :])) * scaling
        dq[...] += dot(qkt[2 * E - EP :, rows], grad_scores)
        dkv_send[:, rows] = jnp.concatenate([grad_key.T[:E], grad_value.T[:E]]).astype(bf16)

    def second_core(i):
        quad = quad_at(i)
        for core in range(2):
            first, second = members(core, quad)
            backward_keys(core * quads + quad)
            unless_me(first, send_dkv)
            unless_me(second, send_dkv)

    each(1, quads, second_core)
    second_core(0 * me)
    dq_send[:, half:] = rows_to(dq[EP - E :, :] * scaling, EP).astype(bf16)

    def send_second(i):
        quad = quad_at(i)
        first, second = members(1, quad)
        unless_me(first, send_dq)
        unless_me(second, send_dq)

    each(1, quads, send_second)
    send_second(0 * me)
    own_dkv = pltpu.make_async_copy(dkv_send.at[:, place_of(me)], dkv_recv.at[me], local_sem.at[3])
    own_dkv.start()
    own_dq = pltpu.make_async_copy(dq_send.at[:, place_of(me)], dq_recv.at[me], local_sem.at[4])
    own_dq.start()

    each(1, nc, lambda j: clip_wait(PRED, pred_recv.at[clip_at(-j)], clip_at(-j)))
    for c in range(nc):
        pred_masked[c] = (pred_recv[c].astype(f32) * receiving[:, c : c + 1]).astype(bf16)
    pred_copy = pltpu.make_async_copy(pred_masked, prediction, local_sem.at[2])
    pred_copy.start()

    def sent_clip(j):
        peer = clip_at(j)
        clip_copy(COT, cot_hbm.at[0, 0, peer], cot_recv.at[clip], peer).wait_send()
        clip_copy(PRED, pred_send, pred_recv.at[clip], peer).wait_send()

    def sent(j):
        peer = seq_at(j)
        seq_copy(QK, qk_send.at[peer], qkt.at[:, place_of(me)], peer).wait_send()
        seq_copy(V, v_send.at[peer], vt.at[:, place_of(me)], peer).wait_send()
        seq_copy(GRADS, grads_send.at[peer], dot_t.at[pl.ds(0, EP), place_of(me)], peer).wait_send()
        seq_copy(DKV, dkv_send.at[:, place_of(peer)], dkv_recv.at[me], peer).wait_send()
        seq_wait(DKV, dkv_recv.at[peer], peer)

    def last(j):
        peer = seq_at(j)
        seq_copy(DQ, dq_send.at[:, place_of(peer)], dq_recv.at[me], peer).wait_send()
        seq_wait(DQ, dq_recv.at[peer], peer)

    each(1, nc, sent_clip)
    own_dkv.wait()
    own_dq.wait()
    pred_copy.wait()
    sent_core(1 + 3, quads, 0)
    sent_core(0, 1, 0)
    sent_core(0, quads, 1)
    each(1, ns, sent)
    each(1, ns, last)


def finish(ns, parts, masked_hbm, dkv_hbm, dq_hbm, prediction, qkv_grad, masked, dkv, dq, xt, turned, sems):
    tiles = qkv_grad.shape[2] // L
    thirds = tiles // 3
    each_part = masked.shape[0] // parts
    dkv_in = pltpu.make_async_copy(dkv_hbm, dkv, sems.at[0])
    dq_in = pltpu.make_async_copy(dq_hbm, dq, sems.at[1])
    dkv_in.start()
    dq_in.start()
    blocks_in, blocks_out = [], []
    for p in range(parts):
        some = pl.ds(p * each_part, each_part)
        blocks_in.append(pltpu.make_async_copy(masked_hbm.at[some], masked.at[some], sems.at[2 + p]))
        blocks_out.append(pltpu.make_async_copy(masked.at[some], prediction.at[0, 0, some], sems.at[2 + parts + p]))
    for copy in blocks_in:
        copy.start()
    dkv_in.wait()
    dq_in.wait()
    for h in range(ns):
        first = 3 * E * h
        xt[first : first + E, :] = dq[h].astype(f32)[:E]
        xt[first + E : first + 3 * E, :] = dkv[h].astype(f32)
    grads_out = []
    for p in range(3):
        for j in range(p * thirds, (p + 1) * thirds):
            turned[:, j * L : (j + 1) * L] = xt[j * L : (j + 1) * L, :].T.astype(bf16)
        columns = pl.ds(p * thirds * L, thirds * L)
        grads_out.append(pltpu.make_async_copy(turned.at[:, columns], qkv_grad.at[0, :, columns], sems.at[2 + 2 * parts + p]))
        grads_out[-1].start()
        for q in range(p * parts // 3, (p + 1) * parts // 3):
            blocks_in[q].wait()
            blocks_out[q].start()
    for copy in blocks_out + grads_out:
        copy.wait()


def on_device(ns, nc, qkv, w_out, enc_gain, w_embed, pred_gain, ctx_blocks, owner, cotangent):
    d, width = w_embed.shape
    tokens = ns * L
    vmem = pl.BlockSpec(memory_space=pltpu.VMEM)
    hbm = pl.BlockSpec(memory_space=pl.ANY)
    scratch = [
        pltpu.VMEM((3 * d + 16, L), f32),
        pltpu.VMEM((L, 3 * d), bf16),
        pltpu.VMEM((d, d), bf16),
        pltpu.VMEM((d, width), bf16),
        pltpu.VMEM((ns, 2 * E, L), bf16),
        pltpu.VMEM((ns, EP, L), bf16),
        pltpu.VMEM((2 * E, tokens), bf16),
        pltpu.VMEM((EP, tokens), bf16),
        pltpu.VMEM((L, tokens), bf16),
        pltpu.VMEM((tokens, L), bf16),
        pltpu.VMEM((tokens, L), bf16),
        pltpu.VMEM((tokens, L), bf16),
        pltpu.VMEM((tokens, tokens), bf16),
        pltpu.VMEM((EP, tokens), bf16),
        pltpu.VMEM((tokens, 2 * L), f32),
        pltpu.VMEM((1, tokens), f32),
        pltpu.VMEM((1, tokens), f32),
        pltpu.VMEM((ns, EP, L), bf16),
        pltpu.VMEM((L, d), bf16),
        pltpu.VMEM((nc, L, width), bf16),
        pltpu.VMEM((L, width), bf16),
        pltpu.VMEM((nc, L, width), bf16),
        pltpu.VMEM((ns, EP, L), bf16),
        pltpu.VMEM((L, tokens), bf16),
        pltpu.VMEM((tokens, L), bf16),
        pltpu.VMEM((EP, tokens // 2), f32),
        pltpu.VMEM((tokens, L), f32),
        pltpu.VMEM((tokens, L), f32),
        pltpu.VMEM((2 * E, tokens), bf16),
        pltpu.VMEM((EP, tokens), bf16),
        pltpu.VMEM((nc, L, width), bf16),
        pltpu.SemaphoreType.DMA((6, ns)),
        pltpu.SemaphoreType.DMA((6, ns)),
        pltpu.SemaphoreType.DMA((2, nc)),
        pltpu.SemaphoreType.DMA((2, nc)),
        pltpu.SemaphoreType.DMA((9,)),
        pltpu.SemaphoreType.REGULAR,
    ]
    prediction, dkv, dq = pl.pallas_call(
        functools.partial(kernel, ns, nc),
        out_shape=(
            jax.ShapeDtypeStruct((nc, L, width), bf16),
            jax.ShapeDtypeStruct((ns, 2 * E, L), bf16),
            jax.ShapeDtypeStruct((ns, EP, L), bf16),
        ),
        in_specs=[hbm, hbm, vmem, hbm, vmem, vmem, vmem, hbm],
        out_specs=(hbm, hbm, hbm),
        scratch_shapes=scratch,
        compiler_params=pltpu.CompilerParams(
            collective_id=0, has_side_effects=True, vmem_limit_bytes=56 * 1024 * 1024
        ),
        cost_estimate=pl.CostEstimate(flops=16_000_000_000, bytes_accessed=12_000_000, transcendentals=4_194_304),
    )(qkv, w_out, enc_gain, w_embed, pred_gain, ctx_blocks.T, owner[None], cotangent)
    parts = min(nc, 4)
    return pl.pallas_call(
        functools.partial(finish, ns, parts),
        out_shape=(
            jax.ShapeDtypeStruct((1, 1, nc, L, width), bf16),
            jax.ShapeDtypeStruct((1, L, 3 * d), bf16),
        ),
        in_specs=[hbm, hbm, hbm],
        out_specs=(hbm, hbm),
        scratch_shapes=[
            pltpu.VMEM((nc, L, width), bf16),
            pltpu.VMEM((ns, 2 * E, L), bf16),
            pltpu.VMEM((ns, EP, L), bf16),
            pltpu.VMEM((3 * d, L), f32),
            pltpu.VMEM((L, 3 * d), bf16),
            pltpu.SemaphoreType.DMA((5 + 2 * parts,)),
        ],
        compiler_params=pltpu.CompilerParams(vmem_limit_bytes=56 * 1024 * 1024),
        cost_estimate=pl.CostEstimate(flops=0, bytes_accessed=6_000_000, transcendentals=0),
    )(prediction, dkv, dq)


def solution(mesh):
    placed = (
        P("clip", "seq", None),
        P(),
        P(),
        P(),
        P(),
        P(),
        P(),
        P("clip", "seq", None, None, None),
    )
    return jax.shard_map(
        functools.partial(on_device, mesh.shape["seq"], mesh.shape["clip"]),
        mesh=mesh,
        in_specs=placed,
        out_specs=(P("clip", "seq", None, None, None), P("clip", "seq", None)),
        check_vma=False,
    )
```

```python
import functools

import jax
import jax.numpy as jnp
from jax import lax
from jax.experimental import pallas as pl
from jax.experimental.pallas import tpu as pltpu
from jax.sharding import PartitionSpec as P

E = 88
EP = 96
L = 128
epsilon = 1e-06
MESH = pl.DeviceIdType.MESH
bf16, f32 = jnp.bfloat16, jnp.float32
contract_last = (((1,), (1,)), ((), ()))

QK, V, HEADS, GRADS, DKV, DQ = range(6)
COT, PRED = range(2)


def dot(a, b):
    return jnp.dot(a, b, preferred_element_type=f32)


def dot_last(a, b):
    return lax.dot_general(a, b, contract_last, preferred_element_type=f32)


def block(index, size=L):
    return pl.ds(pl.multiple_of(index * size, size), size)


def normalize(values):
    average = jnp.mean(values, axis=-1, keepdims=True)
    centred = values - average
    variance = jnp.mean(centred * centred, axis=-1, keepdims=True)
    inverse = lax.rsqrt(variance + epsilon)
    return centred * inverse, inverse


def norm_backward(normed, inverse, upstream):
    average_one = jnp.mean(upstream, axis=-1, keepdims=True)
    average_two = jnp.mean(upstream * normed, axis=-1, keepdims=True)
    return inverse * (upstream - average_one - normed * average_two)


def rows_to(values, rows):
    return jnp.concatenate([values, jnp.zeros((rows - values.shape[0], values.shape[1]), values.dtype)])


def kernel(
    ns,
    nc,
    qkv_hbm,
    w_out_hbm,
    enc_gain,
    w_embed_hbm,
    pred_gain,
    ctx_blocks,
    owner,
    cot_hbm,
    prediction,
    dkv_recv,
    dq_recv,
    xt,
    qkv,
    w_out,
    w_embed,
    qk_send,
    v_send,
    qkt,
    vt,
    qt,
    kn,
    vn,
    qn,
    pt,
    ot,
    score_rows,
    inverse_total,
    correction,
    heads_recv,
    heads_rows,
    cot_recv,
    pred_send,
    pred_recv,
    grads_send,
    dot_t,
    dot_n,
    dq,
    dk_sum,
    dv_sum,
    dkv_send,
    dq_send,
    pred_masked,
    seq_send_sem,
    seq_recv_sem,
    clip_send_sem,
    clip_recv_sem,
    local_sem,
    ready,
):
    me = lax.axis_index("seq")
    clip = lax.axis_index("clip")
    pairs = ns // 2
    my_pair = lax.div(me, 2)
    partner = me + 1 - 2 * lax.rem(me, 2)
    quads = ns // 4
    my_quad = lax.div(me, 4)
    d = ns * E
    tiles = d // L
    width = w_embed_hbm.shape[1]
    scaling = E**-0.5
    to_exp2 = scaling * 1.4426950408889634

    def seq_copy(phase, src, dst, peer):
        return pltpu.make_async_remote_copy(
            src_ref=src,
            dst_ref=dst,
            send_sem=seq_send_sem.at[phase, peer],
            recv_sem=seq_recv_sem.at[phase, me],
            device_id={"seq": peer},
            device_id_type=MESH,
        )

    def seq_wait(phase, dst, source):
        pltpu.make_async_remote_copy(
            src_ref=dst,
            dst_ref=dst,
            send_sem=seq_send_sem.at[phase, source],
            recv_sem=seq_recv_sem.at[phase, source],
            device_id={"seq": source},
            device_id_type=MESH,
        ).wait_recv()

    def clip_copy(phase, src, dst, peer):
        return pltpu.make_async_remote_copy(
            src_ref=src,
            dst_ref=dst,
            send_sem=clip_send_sem.at[phase, peer],
            recv_sem=clip_recv_sem.at[phase, clip],
            device_id={"clip": peer},
            device_id_type=MESH,
        )

    def clip_wait(phase, dst, source):
        pltpu.make_async_remote_copy(
            src_ref=dst,
            dst_ref=dst,
            send_sem=clip_send_sem.at[phase, source],
            recv_sem=clip_recv_sem.at[phase, source],
            device_id={"clip": source},
            device_id_type=MESH,
        ).wait_recv()

    def seq_at(offset):
        return lax.rem(me + offset + ns, ns)

    def pair_at(i, way=1):
        ahead = (pairs // 2 - lax.div(i, 2)) * (1 - 2 * lax.rem(i, 2))
        return lax.rem(my_pair + way * ahead + 2 * pairs, pairs)

    def place_of(source):
        return block(lax.rem(source, 2) * pairs + lax.div(source, 2))

    def quad_at(i):
        ahead = jnp.where(i == 0, 0, (quads // 2 - lax.div(i, 2)) * (1 - 2 * lax.rem(i, 2)))
        return lax.rem(my_quad + ahead + 2 * quads, quads)

    def members(core, quad):
        return 4 * quad + core, 4 * quad + 2 + core

    def unless_me(source, body):
        pl.when(source != me)(lambda: body(source))

    def each_peer(body, way=1):
        def both(i):
            pair = pair_at(i, way)
            body(2 * pair)
            body(2 * pair + 1)

        body(partner)
        each(1, pairs, both)

    def clip_at(offset):
        return lax.rem(clip + offset + nc, nc)

    def each(first, last, body):
        def step(i, carry):
            body(i)
            return carry

        lax.fori_loop(first, last, step, 0)

    qkv_in = []
    for p in range(3):
        columns = pl.ds(p * d, d)
        qkv_in.append(pltpu.make_async_copy(qkv_hbm.at[0, :, columns], qkv.at[:, columns], local_sem.at[5 + p]))
        qkv_in[-1].start()

    barrier = pltpu.get_barrier_semaphore()
    each(1, ns, lambda j: pl.semaphore_signal(barrier, inc=1, device_id={"seq": seq_at(j)}, device_id_type=MESH))
    each(
        clip + 1,
        nc,
        lambda c: pl.semaphore_signal(barrier, inc=1, device_id={"clip": c}, device_id_type=MESH),
    )

    w_out_copy = pltpu.make_async_copy(w_out_hbm, w_out, local_sem.at[0])
    w_out_copy.start()
    w_embed_copy = pltpu.make_async_copy(w_embed_hbm, w_embed, local_sem.at[8])
    w_embed_copy.start()
    own_cot = pltpu.make_async_copy(cot_hbm.at[0, 0, clip], cot_recv.at[clip], local_sem.at[1])
    own_cot.start()

    for p in range(3):
        qkv_in[p].wait()
        for j in range(p * tiles, (p + 1) * tiles):
            xt[j * L : (j + 1) * L, :] = qkv[:, j * L : (j + 1) * L].astype(f32).T
    pl.semaphore_wait(barrier, ns - 1 + clip)
    each(0, clip, lambda c: pl.semaphore_signal(ready, inc=1, device_id={"clip": c}, device_id_type=MESH))

    xt[pl.ds(3 * d, 16), :] = jnp.zeros((16, L), f32)

    def qk_of(h):
        return xt[pl.ds(pl.multiple_of(3 * E * h, 8), 2 * E), :].astype(bf16)

    def v_of(h):
        return xt[pl.ds(pl.multiple_of(3 * E * h + 2 * E, 8), EP), :].astype(bf16)

    def send_qk(peer):
        qk_send[peer] = qk_of(peer)
        seq_copy(QK, qk_send.at[peer], qkt.at[:, place_of(me)], peer).start()

    def send_v(peer):
        v_send[peer] = v_of(peer)
        seq_copy(V, v_send.at[peer], vt.at[:, place_of(me)], peer).start()

    def send_cot(j):
        peer = clip_at(j)
        clip_copy(COT, cot_hbm.at[0, 0, peer], cot_recv.at[clip], peer).start()

    each_peer(send_qk, -1)
    each_peer(send_v, -1)

    qkt[:, place_of(me)] = qk_of(me)
    vt[:, place_of(me)] = v_of(me)
    dot_t[pl.ds(EP, L - EP), :] = jnp.zeros((L - EP, ns * L), bf16)
    dq[...] = jnp.zeros_like(dq)
    dk_sum[...] = jnp.zeros_like(dk_sum)
    dv_sum[...] = jnp.zeros_like(dv_sum)
    masks = owner.shape[1]
    per_clip = masks // nc
    owned = (lax.broadcasted_iota(jnp.int32, (nc, masks), 0) == owner[...]).astype(f32)
    member = jnp.max((ctx_blocks[...] == me).astype(f32), axis=0, keepdims=True)
    mask_id = lax.broadcasted_iota(jnp.int32, (masks, nc), 0)
    first_mask = lax.broadcasted_iota(jnp.int32, (masks, nc), 1) * per_clip
    in_clip = jnp.where((mask_id >= first_mask) & (mask_id < first_mask + per_clip), 1.0, 0.0)
    table = dot(owned * member, in_clip)
    sending = jnp.sum(
        jnp.where(lax.broadcasted_iota(jnp.int32, (nc, nc), 1) == clip, table, 0.0), axis=1, keepdims=True
    )
    receiving = jnp.sum(
        jnp.where(lax.broadcasted_iota(jnp.int32, (nc, nc), 0) == clip, table, 0.0), axis=0, keepdims=True
    )

    def turn_qk(source):
        both = qkt[:, place_of(source)].astype(f32)
        query, key = rows_to(both[:E], L), rows_to(both[E:], L)
        qt[:, place_of(source)] = query.astype(bf16)
        qn[place_of(source), :] = query.T.astype(bf16)
        kn[place_of(source), :] = key.T.astype(bf16)

    turn_qk(me)

    def take_qk(j):
        source = seq_at(-j)
        seq_wait(QK, qkt.at[:, place_of(source)], source)
        turn_qk(source)

    each(7, 10, take_qk)
    pl.when(clip < nc - 1)(lambda: pl.semaphore_wait(ready, nc - 1 - clip))
    each(1, nc, send_cot)
    each(1, 7, take_qk)
    each(10, ns, take_qk)

    def weigh(pair, carry):
        columns = block(pair, 2 * L)
        queries = qt[:, columns]
        largest = None
        for k in range(pairs):
            keys = slice(2 * L * k, 2 * L * (k + 1))
            scores = dot(kn[keys, :], queries)
            score_rows[keys, :] = scores
            part = jnp.max(scores.reshape(2 * L // 8, 8, 2 * L), axis=0)
            largest = part if largest is None else jnp.maximum(largest, part)
        largest = jnp.max(largest, axis=0, keepdims=True)
        total = jnp.zeros((8, 2 * L), f32)
        for k in range(pairs):
            keys = slice(2 * L * k, 2 * L * (k + 1))
            shifted = jnp.exp2((score_rows[keys, :] - largest) * to_exp2)
            total += jnp.sum(shifted.reshape(2 * L // 8, 8, 2 * L), axis=0)
            pt[keys, columns] = shifted.astype(bf16)
        inverse_total[:, columns] = 1.0 / jnp.sum(total, axis=0, keepdims=True)
        return carry

    lax.fori_loop(0, pairs, weigh, 0)

    def wait_v(source):
        seq_wait(V, vt.at[:, place_of(source)], source)

    def turn_v(source):
        vn[place_of(source), :] = rows_to(vt[:, place_of(source)].astype(f32)[:E], L).T.astype(bf16)

    def send_heads(peer):
        seq_copy(HEADS, ot.at[:, place_of(peer)], heads_recv.at[me], peer).start()

    def mix_core(core):
        def step(i):
            quad = quad_at(i)
            first, second = members(core, quad)
            columns = block(core * quads + quad, 2 * L)
            mixed = dot(vt[...], pt[:, columns])[:E] * inverse_total[:, columns]
            ot[:, columns] = rows_to(mixed, EP).astype(bf16)
            unless_me(first, send_heads)
            unless_me(second, send_heads)

        each(1, quads, step)
        step(0 * me)


    def heads_sent(peer):
        seq_copy(HEADS, ot.at[:, place_of(peer)], heads_recv.at[me], peer).wait_send()

    def sent_core(first_i, last_i, core):
        def step(i):
            first, second = members(core, quad_at(i))
            unless_me(first, heads_sent)
            unless_me(second, heads_sent)

        each(first_i, last_i, step)

    each(1, ns, lambda j: wait_v(seq_at(-j)))
    mix_core(0)
    each(0, ns, turn_v)
    sent_core(1, 1 + 3, 0)
    mix_core(1)
    heads_recv[me] = ot[:, place_of(me)]

    own_cot.wait()
    each(1, nc, lambda j: clip_wait(COT, cot_recv.at[clip_at(-j)], clip_at(-j)))
    grad_predicted = jnp.zeros((L, cot_recv.shape[2]), f32)
    for o in range(nc):
        grad_predicted += sending[o : o + 1, :] * cot_recv[o].astype(f32)
    w_out_copy.wait()
    w_embed_copy.wait()

    def take_heads(j):
        source = seq_at(-j)
        seq_wait(HEADS, heads_recv.at[source], source)

    each(1, ns, take_heads)
    for h in range(ns):
        xt[h * E : (h + 1) * E, :] = heads_recv[h].astype(f32)[:E]
    for j in range(tiles):
        heads_rows[:, j * L : (j + 1) * L] = xt[j * L : (j + 1) * L, :].T.astype(bf16)
    encoded = dot(heads_rows[...], w_out[...])
    normed_enc, inverse_enc = normalize(encoded)
    context = (normed_enc * enc_gain[...].reshape(1, d)).astype(bf16)
    embedded = dot(context, w_embed[...])
    normed_emb, inverse_emb = normalize(embedded)
    predicted = (normed_emb * pred_gain[...].reshape(1, width)).astype(bf16)
    pred_send[...] = predicted

    def send_pred(j):
        peer = clip_at(j)
        clip_copy(PRED, pred_send, pred_recv.at[clip], peer).start()

    grad_embedded = norm_backward(normed_emb, inverse_emb, grad_predicted * pred_gain[...].reshape(1, width)).astype(bf16)
    grad_context = dot_last(grad_embedded, w_embed[...])
    grad_encoded = norm_backward(normed_enc, inverse_enc, grad_context * enc_gain[...].reshape(1, d)).astype(bf16)
    xt[0:d, :] = dot_last(w_out[...], grad_encoded)

    def cut_grads(peer):
        grads_send[peer] = xt[pl.ds(pl.multiple_of(peer * E, 8), EP), :].astype(bf16)
        seq_copy(GRADS, grads_send.at[peer], dot_t.at[pl.ds(0, EP), place_of(me)], peer).start()

    each_peer(cut_grads)
    each(1, nc, send_pred)
    dot_t[pl.ds(0, EP), place_of(me)] = xt[pl.ds(pl.multiple_of(me * E, 8), EP), :].astype(bf16)
    pred_recv[clip] = predicted

    def turn_grads(source):
        rounded = (dot_t[:, place_of(source)].astype(f32) * inverse_total[:, place_of(source)]).astype(bf16)
        dot_t[:, place_of(source)] = rounded
        scaled = rounded.astype(f32)
        dot_n[place_of(source), :] = scaled.T.astype(bf16)
        mixed = ot[:, place_of(source)].astype(f32)
        correction[:, place_of(source)] = jnp.sum(scaled[:EP] * mixed, axis=0, keepdims=True)

    def take_grads(source):
        def wait():
            seq_wait(GRADS, dot_t.at[pl.ds(0, EP), place_of(source)], source)

        pl.when(source != me)(wait)
        turn_grads(source)

    def send_dkv(peer):
        seq_copy(DKV, dkv_send.at[:, place_of(peer)], dkv_recv.at[me], peer).start()

    def send_dq(peer):
        seq_copy(DQ, dq_send.at[:, place_of(peer)], dq_recv.at[me], peer).start()

    def backward_queries(pair):
        columns = block(pair, 2 * L)
        grads_t, grads_n, queries = dot_t[:, columns], dot_n[columns, :], qn[columns, :]
        shift = correction[:, columns]
        grad_query = jnp.zeros((EP, 2 * L), f32)
        for k in range(pairs):
            keys = slice(2 * L * k, 2 * L * (k + 1))
            probs = pt[keys, columns]
            grad_probs = dot(vn[keys, :], grads_t)
            grad_scores = (probs.astype(f32) * (grad_probs - shift)).astype(bf16)
            grad_query += dot(qkt[2 * E - EP :, keys], grad_scores)
            dv_sum[keys, :] += dot(probs, grads_n)
            dk_sum[keys, :] += dot(grad_scores, queries)
        dq_send[:, columns] = rows_to(grad_query[EP - E :] * scaling, EP).astype(bf16)

    def first_core(i):
        quad = quad_at(i)
        first, second = members(0, quad)
        take_grads(first)
        take_grads(second)
        backward_queries(quad)
        unless_me(first, send_dq)
        unless_me(second, send_dq)

    each(1, quads, first_core)
    first_core(0 * me)

    def take_second(i):
        quad = quad_at(i)
        first, second = members(1, quad)
        take_grads(first)
        take_grads(second)

    each(0, quads, take_second)
    half = pairs * L

    def backward_keys(pair):
        rows = block(pair, 2 * L)
        probs = pt[rows, half:]
        grad_probs = dot(vn[rows, :], dot_t[:, half:])
        grad_scores = (probs.astype(f32) * (grad_probs - correction[:, half:])).astype(bf16)
        grad_value = dv_sum[rows, :] + dot(probs, dot_n[half:, :])
        grad_key = (dk_sum[rows, :] + dot(grad_scores, qn[half:, :])) * scaling
        dq[...] += dot(qkt[2 * E - EP :, rows], grad_scores)
        dkv_send[:, rows] = jnp.concatenate([grad_key.T[:E], grad_value.T[:E]]).astype(bf16)

    def second_core(i):
        quad = quad_at(i)
        for core in range(2):
            first, second = members(core, quad)
            backward_keys(core * quads + quad)
            unless_me(first, send_dkv)
            unless_me(second, send_dkv)

    each(1, quads, second_core)
    second_core(0 * me)
    dq_send[:, half:] = rows_to(dq[EP - E :, :] * scaling, EP).astype(bf16)

    def send_second(i):
        quad = quad_at(i)
        first, second = members(1, quad)
        unless_me(first, send_dq)
        unless_me(second, send_dq)

    each(1, quads, send_second)
    send_second(0 * me)
    own_dkv = pltpu.make_async_copy(dkv_send.at[:, place_of(me)], dkv_recv.at[me], local_sem.at[3])
    own_dkv.start()
    own_dq = pltpu.make_async_copy(dq_send.at[:, place_of(me)], dq_recv.at[me], local_sem.at[4])
    own_dq.start()

    each(1, nc, lambda j: clip_wait(PRED, pred_recv.at[clip_at(-j)], clip_at(-j)))
    for c in range(nc):
        pred_masked[c] = (pred_recv[c].astype(f32) * receiving[:, c : c + 1]).astype(bf16)
    pred_copy = pltpu.make_async_copy(pred_masked, prediction, local_sem.at[2])
    pred_copy.start()

    def sent_clip(j):
        peer = clip_at(j)
        clip_copy(COT, cot_hbm.at[0, 0, peer], cot_recv.at[clip], peer).wait_send()
        clip_copy(PRED, pred_send, pred_recv.at[clip], peer).wait_send()

    def sent(j):
        peer = seq_at(j)
        seq_copy(QK, qk_send.at[peer], qkt.at[:, place_of(me)], peer).wait_send()
        seq_copy(V, v_send.at[peer], vt.at[:, place_of(me)], peer).wait_send()
        seq_copy(GRADS, grads_send.at[peer], dot_t.at[pl.ds(0, EP), place_of(me)], peer).wait_send()
        seq_copy(DKV, dkv_send.at[:, place_of(peer)], dkv_recv.at[me], peer).wait_send()
        seq_wait(DKV, dkv_recv.at[peer], peer)

    def last(j):
        peer = seq_at(j)
        seq_copy(DQ, dq_send.at[:, place_of(peer)], dq_recv.at[me], peer).wait_send()
        seq_wait(DQ, dq_recv.at[peer], peer)

    each(1, nc, sent_clip)
    own_dkv.wait()
    own_dq.wait()
    pred_copy.wait()
    sent_core(1 + 3, quads, 0)
    sent_core(0, 1, 0)
    sent_core(0, quads, 1)
    each(1, ns, sent)
    each(1, ns, last)


def finish(ns, parts, masked, dkv, dq, prediction, qkv_grad, xt, turned, sems):
    tiles = qkv_grad.shape[2] // L
    thirds = tiles // 3
    each_part = masked.shape[0] // parts
    copies = []
    for p in range(parts):
        some = pl.ds(p * each_part, each_part)
        copies.append(pltpu.make_async_copy(masked.at[some], prediction.at[0, 0, some], sems.at[p]))
        copies[-1].start()
    for h in range(ns):
        first = 3 * E * h
        xt[first : first + E, :] = dq[h].astype(f32)[:E]
        xt[first + E : first + 3 * E, :] = dkv[h].astype(f32)
    for p in range(3):
        for j in range(p * thirds, (p + 1) * thirds):
            turned[:, j * L : (j + 1) * L] = xt[j * L : (j + 1) * L, :].T.astype(bf16)
        columns = pl.ds(p * thirds * L, thirds * L)
        copies.append(pltpu.make_async_copy(turned.at[:, columns], qkv_grad.at[0, :, columns], sems.at[parts + p]))
        copies[-1].start()
    for copy in copies:
        copy.wait()


def on_device(ns, nc, qkv, w_out, enc_gain, w_embed, pred_gain, ctx_blocks, owner, cotangent):
    d, width = w_embed.shape
    tokens = ns * L
    vmem = pl.BlockSpec(memory_space=pltpu.VMEM)
    hbm = pl.BlockSpec(memory_space=pl.ANY)
    scratch = [
        pltpu.VMEM((3 * d + 16, L), f32),
        pltpu.VMEM((L, 3 * d), bf16),
        pltpu.VMEM((d, d), bf16),
        pltpu.VMEM((d, width), bf16),
        pltpu.VMEM((ns, 2 * E, L), bf16),
        pltpu.VMEM((ns, EP, L), bf16),
        pltpu.VMEM((2 * E, tokens), bf16),
        pltpu.VMEM((EP, tokens), bf16),
        pltpu.VMEM((L, tokens), bf16),
        pltpu.VMEM((tokens, L), bf16),
        pltpu.VMEM((tokens, L), bf16),
        pltpu.VMEM((tokens, L), bf16),
        pltpu.VMEM((tokens, tokens), bf16),
        pltpu.VMEM((EP, tokens), bf16),
        pltpu.VMEM((tokens, 2 * L), f32),
        pltpu.VMEM((1, tokens), f32),
        pltpu.VMEM((1, tokens), f32),
        pltpu.VMEM((ns, EP, L), bf16),
        pltpu.VMEM((L, d), bf16),
        pltpu.VMEM((nc, L, width), bf16),
        pltpu.VMEM((L, width), bf16),
        pltpu.VMEM((nc, L, width), bf16),
        pltpu.VMEM((ns, EP, L), bf16),
        pltpu.VMEM((L, tokens), bf16),
        pltpu.VMEM((tokens, L), bf16),
        pltpu.VMEM((EP, tokens // 2), f32),
        pltpu.VMEM((tokens, L), f32),
        pltpu.VMEM((tokens, L), f32),
        pltpu.VMEM((2 * E, tokens), bf16),
        pltpu.VMEM((EP, tokens), bf16),
        pltpu.VMEM((nc, L, width), bf16),
        pltpu.SemaphoreType.DMA((6, ns)),
        pltpu.SemaphoreType.DMA((6, ns)),
        pltpu.SemaphoreType.DMA((2, nc)),
        pltpu.SemaphoreType.DMA((2, nc)),
        pltpu.SemaphoreType.DMA((9,)),
        pltpu.SemaphoreType.REGULAR,
    ]
    prediction, dkv, dq = pl.pallas_call(
        functools.partial(kernel, ns, nc),
        out_shape=(
            pltpu.VMEM((nc, L, width), bf16),
            pltpu.VMEM((ns, 2 * E, L), bf16),
            pltpu.VMEM((ns, EP, L), bf16),
        ),
        in_specs=[hbm, hbm, vmem, hbm, vmem, vmem, vmem, hbm],
        out_specs=(hbm, hbm, hbm),
        scratch_shapes=scratch,
        compiler_params=pltpu.CompilerParams(
            collective_id=0, has_side_effects=True, vmem_limit_bytes=56 * 1024 * 1024
        ),
        cost_estimate=pl.CostEstimate(flops=16_000_000_000, bytes_accessed=12_000_000, transcendentals=4_194_304),
    )(qkv, w_out, enc_gain, w_embed, pred_gain, ctx_blocks.T, owner[None], cotangent)
    parts = min(nc, 4)
    return pl.pallas_call(
        functools.partial(finish, ns, parts),
        out_shape=(
            jax.ShapeDtypeStruct((1, 1, nc, L, width), bf16),
            jax.ShapeDtypeStruct((1, L, 3 * d), bf16),
        ),
        in_specs=[vmem, vmem, vmem],
        out_specs=(hbm, hbm),
        scratch_shapes=[
            pltpu.VMEM((3 * d, L), f32),
            pltpu.VMEM((L, 3 * d), bf16),
            pltpu.SemaphoreType.DMA((3 + parts,)),
        ],
        compiler_params=pltpu.CompilerParams(vmem_limit_bytes=14 * 1024 * 1024),
        cost_estimate=pl.CostEstimate(flops=0, bytes_accessed=6_000_000, transcendentals=0),
    )(prediction, dkv, dq)


def solution(mesh):
    placed = (
        P("clip", "seq", None),
        P(),
        P(),
        P(),
        P(),
        P(),
        P(),
        P("clip", "seq", None, None, None),
    )
    return jax.shard_map(
        functools.partial(on_device, mesh.shape["seq"], mesh.shape["clip"]),
        mesh=mesh,
        in_specs=placed,
        out_specs=(P("clip", "seq", None, None, None), P("clip", "seq", None)),
        check_vma=False,
    )
```

```python
import functools

import jax
import jax.numpy as jnp
from jax import lax
from jax.experimental import pallas as pl
from jax.experimental.pallas import tpu as pltpu
from jax.sharding import PartitionSpec as P

E = 88
EP = 96
L = 128
epsilon = 1e-06
MESH = pl.DeviceIdType.MESH
bf16, f32 = jnp.bfloat16, jnp.float32
contract_last = (((1,), (1,)), ((), ()))

QK, V, HEADS, GRADS, DKV, DQ = range(6)
COT, PRED = range(2)


def dot(a, b):
    return jnp.dot(a, b, preferred_element_type=f32)


def dot_last(a, b):
    return lax.dot_general(a, b, contract_last, preferred_element_type=f32)


def block(index, size=L):
    return pl.ds(pl.multiple_of(index * size, size), size)


def normalize(values):
    average = jnp.mean(values, axis=-1, keepdims=True)
    centred = values - average
    variance = jnp.mean(centred * centred, axis=-1, keepdims=True)
    inverse = lax.rsqrt(variance + epsilon)
    return centred * inverse, inverse


def norm_backward(normed, inverse, upstream):
    average_one = jnp.mean(upstream, axis=-1, keepdims=True)
    average_two = jnp.mean(upstream * normed, axis=-1, keepdims=True)
    return inverse * (upstream - average_one - normed * average_two)


def rows_to(values, rows):
    return jnp.concatenate([values, jnp.zeros((rows - values.shape[0], values.shape[1]), values.dtype)])


def kernel(
    ns,
    nc,
    qkv_hbm,
    w_out_hbm,
    enc_gain,
    w_embed_hbm,
    pred_gain,
    ctx_blocks,
    owner,
    cot_hbm,
    prediction,
    dkv_recv,
    dq_recv,
    xt,
    qkv,
    w_out,
    w_embed,
    qk_send,
    v_send,
    qkt,
    vt,
    qt,
    kn,
    vn,
    qn,
    pt,
    ot,
    score_rows,
    inverse_total,
    correction,
    heads_recv,
    heads_rows,
    cot_recv,
    pred_send,
    pred_recv,
    grads_send,
    dot_t,
    dot_n,
    dq,
    dk_sum,
    dv_sum,
    dkv_send,
    dq_send,
    pred_masked,
    seq_send_sem,
    seq_recv_sem,
    clip_send_sem,
    clip_recv_sem,
    local_sem,
    ready,
):
    me = lax.axis_index("seq")
    clip = lax.axis_index("clip")
    pairs = ns // 2
    my_pair = lax.div(me, 2)
    partner = me + 1 - 2 * lax.rem(me, 2)
    quads = ns // 4
    my_quad = lax.div(me, 4)
    d = ns * E
    tiles = d // L
    width = w_embed_hbm.shape[1]
    scaling = E**-0.5
    to_exp2 = scaling * 1.4426950408889634

    def seq_copy(phase, src, dst, peer):
        return pltpu.make_async_remote_copy(
            src_ref=src,
            dst_ref=dst,
            send_sem=seq_send_sem.at[phase, peer],
            recv_sem=seq_recv_sem.at[phase, me],
            device_id={"seq": peer},
            device_id_type=MESH,
        )

    def seq_wait(phase, dst, source):
        pltpu.make_async_remote_copy(
            src_ref=dst,
            dst_ref=dst,
            send_sem=seq_send_sem.at[phase, source],
            recv_sem=seq_recv_sem.at[phase, source],
            device_id={"seq": source},
            device_id_type=MESH,
        ).wait_recv()

    def clip_copy(phase, src, dst, peer):
        return pltpu.make_async_remote_copy(
            src_ref=src,
            dst_ref=dst,
            send_sem=clip_send_sem.at[phase, peer],
            recv_sem=clip_recv_sem.at[phase, clip],
            device_id={"clip": peer},
            device_id_type=MESH,
        )

    def clip_wait(phase, dst, source):
        pltpu.make_async_remote_copy(
            src_ref=dst,
            dst_ref=dst,
            send_sem=clip_send_sem.at[phase, source],
            recv_sem=clip_recv_sem.at[phase, source],
            device_id={"clip": source},
            device_id_type=MESH,
        ).wait_recv()

    def seq_at(offset):
        return lax.rem(me + offset + ns, ns)

    def pair_at(i, way=1):
        ahead = (pairs // 2 - lax.div(i, 2)) * (1 - 2 * lax.rem(i, 2))
        return lax.rem(my_pair + way * ahead + 2 * pairs, pairs)

    def place_of(source):
        return block(lax.rem(source, 2) * pairs + lax.div(source, 2))

    def quad_at(i):
        ahead = jnp.where(i == 0, 0, (quads // 2 - lax.div(i, 2)) * (1 - 2 * lax.rem(i, 2)))
        return lax.rem(my_quad + ahead + 2 * quads, quads)

    def members(core, quad):
        return 4 * quad + core, 4 * quad + 2 + core

    def unless_me(source, body):
        pl.when(source != me)(lambda: body(source))

    def each_peer(body, way=1):
        def both(i):
            pair = pair_at(i, way)
            body(2 * pair)
            body(2 * pair + 1)

        body(partner)
        each(1, pairs, both)

    def clip_at(offset):
        return lax.rem(clip + offset + nc, nc)

    def each(first, last, body):
        def step(i, carry):
            body(i)
            return carry

        lax.fori_loop(first, last, step, 0)

    qkv_in = []
    for p in range(3):
        columns = pl.ds(p * d, d)
        qkv_in.append(pltpu.make_async_copy(qkv_hbm.at[0, :, columns], qkv.at[:, columns], local_sem.at[5 + p]))
        qkv_in[-1].start()

    barrier = pltpu.get_barrier_semaphore()
    each(1, ns, lambda j: pl.semaphore_signal(barrier, inc=1, device_id={"seq": seq_at(j)}, device_id_type=MESH))
    each(
        clip + 1,
        nc,
        lambda c: pl.semaphore_signal(barrier, inc=1, device_id={"clip": c}, device_id_type=MESH),
    )

    w_out_copy = pltpu.make_async_copy(w_out_hbm, w_out, local_sem.at[0])
    w_out_copy.start()
    w_embed_copy = pltpu.make_async_copy(w_embed_hbm, w_embed, local_sem.at[8])
    w_embed_copy.start()
    own_cot = pltpu.make_async_copy(cot_hbm.at[0, 0, clip], cot_recv.at[clip], local_sem.at[1])
    own_cot.start()

    for p in range(3):
        qkv_in[p].wait()
        for j in range(p * tiles, (p + 1) * tiles):
            xt[j * L : (j + 1) * L, :] = qkv[:, j * L : (j + 1) * L].astype(f32).T
    pl.semaphore_wait(barrier, ns - 1 + clip)
    each(0, clip, lambda c: pl.semaphore_signal(ready, inc=1, device_id={"clip": c}, device_id_type=MESH))

    xt[pl.ds(3 * d, 16), :] = jnp.zeros((16, L), f32)

    def qk_of(h):
        return xt[pl.ds(pl.multiple_of(3 * E * h, 8), 2 * E), :].astype(bf16)

    def v_of(h):
        return xt[pl.ds(pl.multiple_of(3 * E * h + 2 * E, 8), EP), :].astype(bf16)

    def send_qk(peer):
        qk_send[peer] = qk_of(peer)
        seq_copy(QK, qk_send.at[peer], qkt.at[:, place_of(me)], peer).start()

    def send_v(peer):
        v_send[peer] = v_of(peer)
        seq_copy(V, v_send.at[peer], vt.at[:, place_of(me)], peer).start()

    def send_cot(j):
        peer = clip_at(j)
        clip_copy(COT, cot_hbm.at[0, 0, peer], cot_recv.at[clip], peer).start()

    each_peer(send_qk, -1)
    each_peer(send_v, -1)

    qkt[:, place_of(me)] = qk_of(me)
    vt[:, place_of(me)] = v_of(me)
    dot_t[pl.ds(EP, L - EP), :] = jnp.zeros((L - EP, ns * L), bf16)
    dq[...] = jnp.zeros_like(dq)
    dk_sum[...] = jnp.zeros_like(dk_sum)
    dv_sum[...] = jnp.zeros_like(dv_sum)
    masks = owner.shape[1]
    per_clip = masks // nc
    owned = (lax.broadcasted_iota(jnp.int32, (nc, masks), 0) == owner[...]).astype(f32)
    member = jnp.max((ctx_blocks[...] == me).astype(f32), axis=0, keepdims=True)
    mask_id = lax.broadcasted_iota(jnp.int32, (masks, nc), 0)
    first_mask = lax.broadcasted_iota(jnp.int32, (masks, nc), 1) * per_clip
    in_clip = jnp.where((mask_id >= first_mask) & (mask_id < first_mask + per_clip), 1.0, 0.0)
    table = dot(owned * member, in_clip)
    sending = jnp.sum(
        jnp.where(lax.broadcasted_iota(jnp.int32, (nc, nc), 1) == clip, table, 0.0), axis=1, keepdims=True
    )
    receiving = jnp.sum(
        jnp.where(lax.broadcasted_iota(jnp.int32, (nc, nc), 0) == clip, table, 0.0), axis=0, keepdims=True
    )

    def turn_qk(source):
        both = qkt[:, place_of(source)].astype(f32)
        query, key = rows_to(both[:E], L), rows_to(both[E:], L)
        qt[:, place_of(source)] = query.astype(bf16)
        qn[place_of(source), :] = query.T.astype(bf16)
        kn[place_of(source), :] = key.T.astype(bf16)

    turn_qk(me)

    def take_qk(j):
        source = seq_at(-j)
        seq_wait(QK, qkt.at[:, place_of(source)], source)
        turn_qk(source)

    each(7, 10, take_qk)
    pl.when(clip < nc - 1)(lambda: pl.semaphore_wait(ready, nc - 1 - clip))
    each(1, nc, send_cot)
    each(1, 7, take_qk)
    each(10, ns, take_qk)

    def weigh(pair, carry):
        columns = block(pair, 2 * L)
        queries = qt[:, columns]
        largest = None
        for k in range(pairs):
            keys = slice(2 * L * k, 2 * L * (k + 1))
            scores = dot(kn[keys, :], queries)
            score_rows[keys, :] = scores
            part = jnp.max(scores.reshape(2 * L // 8, 8, 2 * L), axis=0)
            largest = part if largest is None else jnp.maximum(largest, part)
        largest = jnp.max(largest, axis=0, keepdims=True)
        total = jnp.zeros((8, 2 * L), f32)
        for k in range(pairs):
            keys = slice(2 * L * k, 2 * L * (k + 1))
            shifted = jnp.exp2((score_rows[keys, :] - largest) * to_exp2)
            total += jnp.sum(shifted.reshape(2 * L // 8, 8, 2 * L), axis=0)
            pt[keys, columns] = shifted.astype(bf16)
        inverse_total[:, columns] = 1.0 / jnp.sum(total, axis=0, keepdims=True)
        return carry

    lax.fori_loop(0, pairs, weigh, 0)

    def wait_v(source):
        seq_wait(V, vt.at[:, place_of(source)], source)

    def turn_v(source):
        vn[place_of(source), :] = rows_to(vt[:, place_of(source)].astype(f32)[:E], L).T.astype(bf16)

    def send_heads(peer):
        seq_copy(HEADS, ot.at[:, place_of(peer)], heads_recv.at[me], peer).start()

    def mix_core(core):
        def step(i):
            quad = quad_at(i)
            first, second = members(core, quad)
            columns = block(core * quads + quad, 2 * L)
            mixed = dot(vt[...], pt[:, columns])[:E] * inverse_total[:, columns]
            ot[:, columns] = rows_to(mixed, EP).astype(bf16)
            unless_me(first, send_heads)
            unless_me(second, send_heads)

        each(1, quads, step)
        step(0 * me)


    def heads_sent(peer):
        seq_copy(HEADS, ot.at[:, place_of(peer)], heads_recv.at[me], peer).wait_send()

    def sent_core(first_i, last_i, core):
        def step(i):
            first, second = members(core, quad_at(i))
            unless_me(first, heads_sent)
            unless_me(second, heads_sent)

        each(first_i, last_i, step)

    each(1, ns, lambda j: wait_v(seq_at(-j)))
    mix_core(0)
    each(0, ns, turn_v)
    sent_core(1, 1 + 3, 0)
    mix_core(1)
    heads_recv[me] = ot[:, place_of(me)]

    own_cot.wait()
    each(1, nc, lambda j: clip_wait(COT, cot_recv.at[clip_at(-j)], clip_at(-j)))
    grad_predicted = jnp.zeros((L, cot_recv.shape[2]), f32)
    for o in range(nc):
        grad_predicted += sending[o : o + 1, :] * cot_recv[o].astype(f32)
    w_out_copy.wait()
    w_embed_copy.wait()

    def take_heads(j):
        source = seq_at(-j)
        seq_wait(HEADS, heads_recv.at[source], source)

    each(1, ns, take_heads)
    for h in range(ns):
        xt[h * E : (h + 1) * E, :] = heads_recv[h].astype(f32)[:E]
    for j in range(tiles):
        heads_rows[:, j * L : (j + 1) * L] = xt[j * L : (j + 1) * L, :].T.astype(bf16)
    encoded = dot(heads_rows[...], w_out[...])
    normed_enc, inverse_enc = normalize(encoded)
    context = (normed_enc * enc_gain[...].reshape(1, d)).astype(bf16)
    embedded = dot(context, w_embed[...])
    normed_emb, inverse_emb = normalize(embedded)
    predicted = (normed_emb * pred_gain[...].reshape(1, width)).astype(bf16)
    pred_send[...] = predicted

    def send_pred(j):
        peer = clip_at(j)
        clip_copy(PRED, pred_send, pred_recv.at[clip], peer).start()

    grad_embedded = norm_backward(normed_emb, inverse_emb, grad_predicted * pred_gain[...].reshape(1, width)).astype(bf16)
    grad_context = dot_last(grad_embedded, w_embed[...])
    grad_encoded = norm_backward(normed_enc, inverse_enc, grad_context * enc_gain[...].reshape(1, d)).astype(bf16)
    xt[0:d, :] = dot_last(w_out[...], grad_encoded)

    def cut_grads(peer):
        grads_send[peer] = xt[pl.ds(pl.multiple_of(peer * E, 8), EP), :].astype(bf16)
        seq_copy(GRADS, grads_send.at[peer], dot_t.at[pl.ds(0, EP), place_of(me)], peer).start()

    each_peer(cut_grads)
    each(1, nc, send_pred)
    dot_t[pl.ds(0, EP), place_of(me)] = xt[pl.ds(pl.multiple_of(me * E, 8), EP), :].astype(bf16)
    pred_recv[clip] = predicted

    def turn_grads(source):
        rounded = (dot_t[:, place_of(source)].astype(f32) * inverse_total[:, place_of(source)]).astype(bf16)
        dot_t[:, place_of(source)] = rounded
        scaled = rounded.astype(f32)
        dot_n[place_of(source), :] = scaled.T.astype(bf16)
        mixed = ot[:, place_of(source)].astype(f32)
        correction[:, place_of(source)] = jnp.sum(scaled[:EP] * mixed, axis=0, keepdims=True)

    def take_grads(source):
        def wait():
            seq_wait(GRADS, dot_t.at[pl.ds(0, EP), place_of(source)], source)

        pl.when(source != me)(wait)
        turn_grads(source)

    def send_dkv(peer):
        seq_copy(DKV, dkv_send.at[:, place_of(peer)], dkv_recv.at[me], peer).start()

    def send_dq(peer):
        seq_copy(DQ, dq_send.at[:, place_of(peer)], dq_recv.at[me], peer).start()

    def backward_queries(pair):
        columns = block(pair, 2 * L)
        grads_t, grads_n, queries = dot_t[:, columns], dot_n[columns, :], qn[columns, :]
        shift = correction[:, columns]
        grad_query = jnp.zeros((EP, 2 * L), f32)
        for k in range(pairs):
            keys = slice(2 * L * k, 2 * L * (k + 1))
            probs = pt[keys, columns]
            grad_probs = dot(vn[keys, :], grads_t)
            grad_scores = (probs.astype(f32) * (grad_probs - shift)).astype(bf16)
            grad_query += dot(qkt[2 * E - EP :, keys], grad_scores)
            dv_sum[keys, :] += dot(probs, grads_n)
            dk_sum[keys, :] += dot(grad_scores, queries)
        dq_send[:, columns] = rows_to(grad_query[EP - E :] * scaling, EP).astype(bf16)

    def first_core(i):
        quad = quad_at(i)
        first, second = members(0, quad)
        take_grads(first)
        take_grads(second)
        backward_queries(quad)
        unless_me(first, send_dq)
        unless_me(second, send_dq)

    each(1, quads, first_core)
    first_core(0 * me)

    def take_second(i):
        quad = quad_at(i)
        first, second = members(1, quad)
        take_grads(first)
        take_grads(second)

    each(0, quads, take_second)
    half = pairs * L

    def backward_keys(pair):
        rows = block(pair, 2 * L)
        probs = pt[rows, half:]
        grad_probs = dot(vn[rows, :], dot_t[:, half:])
        grad_scores = (probs.astype(f32) * (grad_probs - correction[:, half:])).astype(bf16)
        grad_value = dv_sum[rows, :] + dot(probs, dot_n[half:, :])
        grad_key = (dk_sum[rows, :] + dot(grad_scores, qn[half:, :])) * scaling
        dq[...] += dot(qkt[2 * E - EP :, rows], grad_scores)
        dkv_send[:, rows] = jnp.concatenate([grad_key.T[:E], grad_value.T[:E]]).astype(bf16)

    def second_core(i):
        quad = quad_at(i)
        for core in range(2):
            first, second = members(core, quad)
            backward_keys(core * quads + quad)
            unless_me(first, send_dkv)
            unless_me(second, send_dkv)

    each(1, quads, second_core)
    second_core(0 * me)
    dq_send[:, half:] = rows_to(dq[EP - E :, :] * scaling, EP).astype(bf16)

    def send_second(i):
        quad = quad_at(i)
        first, second = members(1, quad)
        unless_me(first, send_dq)
        unless_me(second, send_dq)

    send_second(0 * me)
    each(1, quads, send_second)
    own_dkv = pltpu.make_async_copy(dkv_send.at[:, place_of(me)], dkv_recv.at[me], local_sem.at[3])
    own_dkv.start()
    own_dq = pltpu.make_async_copy(dq_send.at[:, place_of(me)], dq_recv.at[me], local_sem.at[4])
    own_dq.start()

    each(1, nc, lambda j: clip_wait(PRED, pred_recv.at[clip_at(-j)], clip_at(-j)))
    for c in range(nc):
        pred_masked[c] = (pred_recv[c].astype(f32) * receiving[:, c : c + 1]).astype(bf16)
    pred_copy = pltpu.make_async_copy(pred_masked, prediction, local_sem.at[2])
    pred_copy.start()

    def sent_clip(j):
        peer = clip_at(j)
        clip_copy(COT, cot_hbm.at[0, 0, peer], cot_recv.at[clip], peer).wait_send()
        clip_copy(PRED, pred_send, pred_recv.at[clip], peer).wait_send()

    def sent(j):
        peer = seq_at(j)
        seq_copy(QK, qk_send.at[peer], qkt.at[:, place_of(me)], peer).wait_send()
        seq_copy(V, v_send.at[peer], vt.at[:, place_of(me)], peer).wait_send()
        seq_copy(GRADS, grads_send.at[peer], dot_t.at[pl.ds(0, EP), place_of(me)], peer).wait_send()
        seq_copy(DKV, dkv_send.at[:, place_of(peer)], dkv_recv.at[me], peer).wait_send()
        seq_wait(DKV, dkv_recv.at[peer], peer)

    def last(j):
        peer = seq_at(j)
        seq_copy(DQ, dq_send.at[:, place_of(peer)], dq_recv.at[me], peer).wait_send()
        seq_wait(DQ, dq_recv.at[peer], peer)

    each(1, nc, sent_clip)
    own_dkv.wait()
    own_dq.wait()
    pred_copy.wait()
    sent_core(1 + 3, quads, 0)
    sent_core(0, 1, 0)
    sent_core(0, quads, 1)
    each(1, ns, sent)
    each(1, ns, last)


def finish(ns, parts, masked, dkv, dq, prediction, qkv_grad, xt, turned, sems):
    tiles = qkv_grad.shape[2] // L
    thirds = tiles // 3
    each_part = masked.shape[0] // parts
    copies = []
    for p in range(parts):
        some = pl.ds(p * each_part, each_part)
        copies.append(pltpu.make_async_copy(masked.at[some], prediction.at[0, 0, some], sems.at[p]))
        copies[-1].start()
    for h in range(ns):
        first = 3 * E * h
        xt[first : first + E, :] = dq[h].astype(f32)[:E]
        xt[first + E : first + 3 * E, :] = dkv[h].astype(f32)
    for p in range(3):
        for j in range(p * thirds, (p + 1) * thirds):
            turned[:, j * L : (j + 1) * L] = xt[j * L : (j + 1) * L, :].T.astype(bf16)
        columns = pl.ds(p * thirds * L, thirds * L)
        copies.append(pltpu.make_async_copy(turned.at[:, columns], qkv_grad.at[0, :, columns], sems.at[parts + p]))
        copies[-1].start()
    for copy in copies:
        copy.wait()


def on_device(ns, nc, qkv, w_out, enc_gain, w_embed, pred_gain, ctx_blocks, owner, cotangent):
    d, width = w_embed.shape
    tokens = ns * L
    vmem = pl.BlockSpec(memory_space=pltpu.VMEM)
    hbm = pl.BlockSpec(memory_space=pl.ANY)
    scratch = [
        pltpu.VMEM((3 * d + 16, L), f32),
        pltpu.VMEM((L, 3 * d), bf16),
        pltpu.VMEM((d, d), bf16),
        pltpu.VMEM((d, width), bf16),
        pltpu.VMEM((ns, 2 * E, L), bf16),
        pltpu.VMEM((ns, EP, L), bf16),
        pltpu.VMEM((2 * E, tokens), bf16),
        pltpu.VMEM((EP, tokens), bf16),
        pltpu.VMEM((L, tokens), bf16),
        pltpu.VMEM((tokens, L), bf16),
        pltpu.VMEM((tokens, L), bf16),
        pltpu.VMEM((tokens, L), bf16),
        pltpu.VMEM((tokens, tokens), bf16),
        pltpu.VMEM((EP, tokens), bf16),
        pltpu.VMEM((tokens, 2 * L), f32),
        pltpu.VMEM((1, tokens), f32),
        pltpu.VMEM((1, tokens), f32),
        pltpu.VMEM((ns, EP, L), bf16),
        pltpu.VMEM((L, d), bf16),
        pltpu.VMEM((nc, L, width), bf16),
        pltpu.VMEM((L, width), bf16),
        pltpu.VMEM((nc, L, width), bf16),
        pltpu.VMEM((ns, EP, L), bf16),
        pltpu.VMEM((L, tokens), bf16),
        pltpu.VMEM((tokens, L), bf16),
        pltpu.VMEM((EP, tokens // 2), f32),
        pltpu.VMEM((tokens, L), f32),
        pltpu.VMEM((tokens, L), f32),
        pltpu.VMEM((2 * E, tokens), bf16),
        pltpu.VMEM((EP, tokens), bf16),
        pltpu.VMEM((nc, L, width), bf16),
        pltpu.SemaphoreType.DMA((6, ns)),
        pltpu.SemaphoreType.DMA((6, ns)),
        pltpu.SemaphoreType.DMA((2, nc)),
        pltpu.SemaphoreType.DMA((2, nc)),
        pltpu.SemaphoreType.DMA((9,)),
        pltpu.SemaphoreType.REGULAR,
    ]
    prediction, dkv, dq = pl.pallas_call(
        functools.partial(kernel, ns, nc),
        out_shape=(
            pltpu.VMEM((nc, L, width), bf16),
            pltpu.VMEM((ns, 2 * E, L), bf16),
            pltpu.VMEM((ns, EP, L), bf16),
        ),
        in_specs=[hbm, hbm, vmem, hbm, vmem, vmem, vmem, hbm],
        out_specs=(hbm, hbm, hbm),
        scratch_shapes=scratch,
        compiler_params=pltpu.CompilerParams(
            collective_id=0, has_side_effects=True, vmem_limit_bytes=56 * 1024 * 1024
        ),
        cost_estimate=pl.CostEstimate(flops=16_000_000_000, bytes_accessed=12_000_000, transcendentals=4_194_304),
    )(qkv, w_out, enc_gain, w_embed, pred_gain, ctx_blocks.T, owner[None], cotangent)
    parts = min(nc, 4)
    return pl.pallas_call(
        functools.partial(finish, ns, parts),
        out_shape=(
            jax.ShapeDtypeStruct((1, 1, nc, L, width), bf16),
            jax.ShapeDtypeStruct((1, L, 3 * d), bf16),
        ),
        in_specs=[vmem, vmem, vmem],
        out_specs=(hbm, hbm),
        scratch_shapes=[
            pltpu.VMEM((3 * d, L), f32),
            pltpu.VMEM((L, 3 * d), bf16),
            pltpu.SemaphoreType.DMA((3 + parts,)),
        ],
        compiler_params=pltpu.CompilerParams(vmem_limit_bytes=14 * 1024 * 1024),
        cost_estimate=pl.CostEstimate(flops=0, bytes_accessed=6_000_000, transcendentals=0),
    )(prediction, dkv, dq)


def solution(mesh):
    placed = (
        P("clip", "seq", None),
        P(),
        P(),
        P(),
        P(),
        P(),
        P(),
        P("clip", "seq", None, None, None),
    )
    return jax.shard_map(
        functools.partial(on_device, mesh.shape["seq"], mesh.shape["clip"]),
        mesh=mesh,
        in_specs=placed,
        out_specs=(P("clip", "seq", None, None, None), P("clip", "seq", None)),
        check_vma=False,
    )
```

```python
import functools

import jax
import jax.numpy as jnp
from jax import lax
from jax.experimental import pallas as pl
from jax.experimental.pallas import tpu as pltpu
from jax.sharding import PartitionSpec as P

E = 88
EP = 96
L = 128
epsilon = 1e-06
MESH = pl.DeviceIdType.MESH
bf16, f32 = jnp.bfloat16, jnp.float32
contract_last = (((1,), (1,)), ((), ()))

QK, V, HEADS, GRADS, DKV, DQ = range(6)
COT, PRED = range(2)


def dot(a, b):
    return jnp.dot(a, b, preferred_element_type=f32)


def dot_last(a, b):
    return lax.dot_general(a, b, contract_last, preferred_element_type=f32)


def block(index, size=L):
    return pl.ds(pl.multiple_of(index * size, size), size)


def normalize(values):
    average = jnp.mean(values, axis=-1, keepdims=True)
    centred = values - average
    variance = jnp.mean(centred * centred, axis=-1, keepdims=True)
    inverse = lax.rsqrt(variance + epsilon)
    return centred * inverse, inverse


def norm_backward(normed, inverse, upstream):
    average_one = jnp.mean(upstream, axis=-1, keepdims=True)
    average_two = jnp.mean(upstream * normed, axis=-1, keepdims=True)
    return inverse * (upstream - average_one - normed * average_two)


def rows_to(values, rows):
    return jnp.concatenate([values, jnp.zeros((rows - values.shape[0], values.shape[1]), values.dtype)])


def kernel(
    ns,
    nc,
    qkv_hbm,
    w_out_hbm,
    enc_gain,
    w_embed_hbm,
    pred_gain,
    ctx_blocks,
    owner,
    cot_hbm,
    prediction,
    dkv_recv,
    dq_recv,
    xt,
    qkv,
    w_out,
    w_embed,
    qk_send,
    v_send,
    qkt,
    vt,
    qt,
    kn,
    vn,
    qn,
    pt,
    ot,
    score_rows,
    inverse_total,
    correction,
    heads_recv,
    heads_rows,
    cot_recv,
    pred_send,
    pred_recv,
    grads_send,
    dot_t,
    dot_n,
    dq,
    dk_sum,
    dv_sum,
    dkv_send,
    dq_send,
    seq_send_sem,
    seq_recv_sem,
    clip_send_sem,
    clip_recv_sem,
    local_sem,
    ready,
):
    me = lax.axis_index("seq")
    clip = lax.axis_index("clip")
    pairs = ns // 2
    my_pair = lax.div(me, 2)
    partner = me + 1 - 2 * lax.rem(me, 2)
    quads = ns // 4
    my_quad = lax.div(me, 4)
    d = ns * E
    tiles = d // L
    width = w_embed_hbm.shape[1]
    scaling = E**-0.5
    to_exp2 = scaling * 1.4426950408889634

    def seq_copy(phase, src, dst, peer):
        return pltpu.make_async_remote_copy(
            src_ref=src,
            dst_ref=dst,
            send_sem=seq_send_sem.at[phase, peer],
            recv_sem=seq_recv_sem.at[phase, me],
            device_id={"seq": peer},
            device_id_type=MESH,
        )

    def seq_wait(phase, dst, source):
        pltpu.make_async_remote_copy(
            src_ref=dst,
            dst_ref=dst,
            send_sem=seq_send_sem.at[phase, source],
            recv_sem=seq_recv_sem.at[phase, source],
            device_id={"seq": source},
            device_id_type=MESH,
        ).wait_recv()

    def clip_copy(phase, src, dst, peer):
        return pltpu.make_async_remote_copy(
            src_ref=src,
            dst_ref=dst,
            send_sem=clip_send_sem.at[phase, peer],
            recv_sem=clip_recv_sem.at[phase, clip],
            device_id={"clip": peer},
            device_id_type=MESH,
        )

    def clip_wait(phase, dst, source):
        pltpu.make_async_remote_copy(
            src_ref=dst,
            dst_ref=dst,
            send_sem=clip_send_sem.at[phase, source],
            recv_sem=clip_recv_sem.at[phase, source],
            device_id={"clip": source},
            device_id_type=MESH,
        ).wait_recv()

    def seq_at(offset):
        return lax.rem(me + offset + ns, ns)

    def pair_at(i, way=1):
        ahead = (pairs // 2 - lax.div(i, 2)) * (1 - 2 * lax.rem(i, 2))
        return lax.rem(my_pair + way * ahead + 2 * pairs, pairs)

    def place_of(source):
        return block(lax.rem(source, 2) * pairs + lax.div(source, 2))

    def quad_at(i):
        ahead = jnp.where(i == 0, 0, (quads // 2 - lax.div(i, 2)) * (1 - 2 * lax.rem(i, 2)))
        return lax.rem(my_quad + ahead + 2 * quads, quads)

    def members(core, quad):
        return 4 * quad + core, 4 * quad + 2 + core

    def unless_me(source, body):
        pl.when(source != me)(lambda: body(source))

    def each_peer(body, way=1):
        def both(i):
            pair = pair_at(i, way)
            body(2 * pair)
            body(2 * pair + 1)

        body(partner)
        each(1, pairs, both)

    def clip_at(offset):
        return lax.rem(clip + offset + nc, nc)

    def each(first, last, body):
        def step(i, carry):
            body(i)
            return carry

        lax.fori_loop(first, last, step, 0)

    qkv_in = []
    for p in range(3):
        columns = pl.ds(p * d, d)
        qkv_in.append(pltpu.make_async_copy(qkv_hbm.at[0, :, columns], qkv.at[:, columns], local_sem.at[5 + p]))
        qkv_in[-1].start()

    barrier = pltpu.get_barrier_semaphore()
    each(1, ns, lambda j: pl.semaphore_signal(barrier, inc=1, device_id={"seq": seq_at(j)}, device_id_type=MESH))
    each(
        clip + 1,
        nc,
        lambda c: pl.semaphore_signal(barrier, inc=1, device_id={"clip": c}, device_id_type=MESH),
    )

    w_out_copy = pltpu.make_async_copy(w_out_hbm, w_out, local_sem.at[0])
    w_out_copy.start()
    w_embed_copy = pltpu.make_async_copy(w_embed_hbm, w_embed, local_sem.at[8])
    w_embed_copy.start()
    own_cot = pltpu.make_async_copy(cot_hbm.at[0, 0, clip], cot_recv.at[clip], local_sem.at[1])
    own_cot.start()

    for p in range(3):
        qkv_in[p].wait()
        for j in range(p * tiles, (p + 1) * tiles):
            xt[j * L : (j + 1) * L, :] = qkv[:, j * L : (j + 1) * L].astype(f32).T
    pl.semaphore_wait(barrier, ns - 1 + clip)
    each(0, clip, lambda c: pl.semaphore_signal(ready, inc=1, device_id={"clip": c}, device_id_type=MESH))

    xt[pl.ds(3 * d, 16), :] = jnp.zeros((16, L), f32)

    def qk_of(h):
        return xt[pl.ds(pl.multiple_of(3 * E * h, 8), 2 * E), :].astype(bf16)

    def v_of(h):
        return xt[pl.ds(pl.multiple_of(3 * E * h + 2 * E, 8), EP), :].astype(bf16)

    def send_qk(peer):
        qk_send[peer] = qk_of(peer)
        seq_copy(QK, qk_send.at[peer], qkt.at[:, place_of(me)], peer).start()

    def send_v(peer):
        v_send[peer] = v_of(peer)
        seq_copy(V, v_send.at[peer], vt.at[:, place_of(me)], peer).start()

    def send_cot(j):
        peer = clip_at(j)
        clip_copy(COT, cot_hbm.at[0, 0, peer], cot_recv.at[clip], peer).start()

    each_peer(send_qk, -1)
    each_peer(send_v, -1)

    qkt[:, place_of(me)] = qk_of(me)
    vt[:, place_of(me)] = v_of(me)
    dot_t[pl.ds(EP, L - EP), :] = jnp.zeros((L - EP, ns * L), bf16)
    dq[...] = jnp.zeros_like(dq)
    dk_sum[...] = jnp.zeros_like(dk_sum)
    dv_sum[...] = jnp.zeros_like(dv_sum)
    masks = owner.shape[1]
    per_clip = masks // nc
    owned = (lax.broadcasted_iota(jnp.int32, (nc, masks), 0) == owner[...]).astype(f32)
    member = jnp.max((ctx_blocks[...] == me).astype(f32), axis=0, keepdims=True)
    mask_id = lax.broadcasted_iota(jnp.int32, (masks, nc), 0)
    first_mask = lax.broadcasted_iota(jnp.int32, (masks, nc), 1) * per_clip
    in_clip = jnp.where((mask_id >= first_mask) & (mask_id < first_mask + per_clip), 1.0, 0.0)
    table = dot(owned * member, in_clip)
    sending = jnp.sum(
        jnp.where(lax.broadcasted_iota(jnp.int32, (nc, nc), 1) == clip, table, 0.0), axis=1, keepdims=True
    )
    receiving = jnp.sum(
        jnp.where(lax.broadcasted_iota(jnp.int32, (nc, nc), 0) == clip, table, 0.0), axis=0, keepdims=True
    )

    def turn_qk(source):
        both = qkt[:, place_of(source)].astype(f32)
        query, key = rows_to(both[:E], L), rows_to(both[E:], L)
        qt[:, place_of(source)] = query.astype(bf16)
        qn[place_of(source), :] = query.T.astype(bf16)
        kn[place_of(source), :] = key.T.astype(bf16)

    turn_qk(me)

    def take_qk(j):
        source = seq_at(-j)
        seq_wait(QK, qkt.at[:, place_of(source)], source)
        turn_qk(source)

    each(7, 10, take_qk)
    pl.when(clip < nc - 1)(lambda: pl.semaphore_wait(ready, nc - 1 - clip))
    each(1, nc, send_cot)
    each(1, 7, take_qk)
    each(10, ns, take_qk)

    def weigh(pair, carry):
        columns = block(pair, 2 * L)
        queries = qt[:, columns]
        largest = None
        for k in range(pairs):
            keys = slice(2 * L * k, 2 * L * (k + 1))
            scores = dot(kn[keys, :], queries)
            score_rows[keys, :] = scores
            part = jnp.max(scores.reshape(2 * L // 8, 8, 2 * L), axis=0)
            largest = part if largest is None else jnp.maximum(largest, part)
        largest = jnp.max(largest, axis=0, keepdims=True)
        total = jnp.zeros((8, 2 * L), f32)
        for k in range(pairs):
            keys = slice(2 * L * k, 2 * L * (k + 1))
            shifted = jnp.exp2((score_rows[keys, :] - largest) * to_exp2)
            total += jnp.sum(shifted.reshape(2 * L // 8, 8, 2 * L), axis=0)
            pt[keys, columns] = shifted.astype(bf16)
        inverse_total[:, columns] = 1.0 / jnp.sum(total, axis=0, keepdims=True)
        return carry

    lax.fori_loop(0, pairs, weigh, 0)

    def wait_v(source):
        seq_wait(V, vt.at[:, place_of(source)], source)

    def turn_v(source):
        vn[place_of(source), :] = rows_to(vt[:, place_of(source)].astype(f32)[:E], L).T.astype(bf16)

    def send_heads(peer):
        seq_copy(HEADS, ot.at[:, place_of(peer)], heads_recv.at[me], peer).start()

    def mix_core(core):
        def step(i):
            quad = quad_at(i)
            first, second = members(core, quad)
            columns = block(core * quads + quad, 2 * L)
            mixed = dot(vt[...], pt[:, columns])[:E] * inverse_total[:, columns]
            ot[:, columns] = rows_to(mixed, EP).astype(bf16)
            unless_me(first, send_heads)
            unless_me(second, send_heads)

        each(1, quads, step)
        step(0 * me)


    def heads_sent(peer):
        seq_copy(HEADS, ot.at[:, place_of(peer)], heads_recv.at[me], peer).wait_send()

    def sent_core(first_i, last_i, core):
        def step(i):
            first, second = members(core, quad_at(i))
            unless_me(first, heads_sent)
            unless_me(second, heads_sent)

        each(first_i, last_i, step)

    each(1, ns, lambda j: wait_v(seq_at(-j)))
    mix_core(0)
    each(0, ns, turn_v)
    sent_core(1, 1 + 3, 0)
    mix_core(1)
    heads_recv[me] = ot[:, place_of(me)]

    own_cot.wait()
    each(1, nc, lambda j: clip_wait(COT, cot_recv.at[clip_at(-j)], clip_at(-j)))
    grad_predicted = jnp.zeros((L, cot_recv.shape[2]), f32)
    for o in range(nc):
        grad_predicted += sending[o : o + 1, :] * cot_recv[o].astype(f32)
    w_out_copy.wait()
    w_embed_copy.wait()

    def take_heads(j):
        source = seq_at(-j)
        seq_wait(HEADS, heads_recv.at[source], source)

    each(1, ns, take_heads)
    for h in range(ns):
        xt[h * E : (h + 1) * E, :] = heads_recv[h].astype(f32)[:E]
    for j in range(tiles):
        heads_rows[:, j * L : (j + 1) * L] = xt[j * L : (j + 1) * L, :].T.astype(bf16)
    encoded = dot(heads_rows[...], w_out[...])
    normed_enc, inverse_enc = normalize(encoded)
    context = (normed_enc * enc_gain[...].reshape(1, d)).astype(bf16)
    embedded = dot(context, w_embed[...])
    normed_emb, inverse_emb = normalize(embedded)
    predicted = (normed_emb * pred_gain[...].reshape(1, width)).astype(bf16)
    pred_send[...] = predicted

    def send_pred(j):
        peer = clip_at(j)
        clip_copy(PRED, pred_send, pred_recv.at[clip], peer).start()

    grad_embedded = norm_backward(normed_emb, inverse_emb, grad_predicted * pred_gain[...].reshape(1, width)).astype(bf16)
    grad_context = dot_last(grad_embedded, w_embed[...])
    grad_encoded = norm_backward(normed_enc, inverse_enc, grad_context * enc_gain[...].reshape(1, d)).astype(bf16)
    xt[0:d, :] = dot_last(w_out[...], grad_encoded)

    def cut_grads(peer):
        grads_send[peer] = xt[pl.ds(pl.multiple_of(peer * E, 8), EP), :].astype(bf16)
        seq_copy(GRADS, grads_send.at[peer], dot_t.at[pl.ds(0, EP), place_of(me)], peer).start()

    each_peer(cut_grads)
    each(1, nc, send_pred)
    dot_t[pl.ds(0, EP), place_of(me)] = xt[pl.ds(pl.multiple_of(me * E, 8), EP), :].astype(bf16)
    pred_recv[clip] = predicted

    def turn_grads(source):
        rounded = (dot_t[:, place_of(source)].astype(f32) * inverse_total[:, place_of(source)]).astype(bf16)
        dot_t[:, place_of(source)] = rounded
        scaled = rounded.astype(f32)
        dot_n[place_of(source), :] = scaled.T.astype(bf16)
        mixed = ot[:, place_of(source)].astype(f32)
        correction[:, place_of(source)] = jnp.sum(scaled[:EP] * mixed, axis=0, keepdims=True)

    def take_grads(source):
        def wait():
            seq_wait(GRADS, dot_t.at[pl.ds(0, EP), place_of(source)], source)

        pl.when(source != me)(wait)
        turn_grads(source)

    def send_dkv(peer):
        seq_copy(DKV, dkv_send.at[:, place_of(peer)], dkv_recv.at[me], peer).start()

    def send_dq(peer):
        seq_copy(DQ, dq_send.at[:, place_of(peer)], dq_recv.at[me], peer).start()

    def backward_queries(pair):
        columns = block(pair, 2 * L)
        grads_t, grads_n, queries = dot_t[:, columns], dot_n[columns, :], qn[columns, :]
        shift = correction[:, columns]
        grad_query = jnp.zeros((EP, 2 * L), f32)
        for k in range(pairs):
            keys = slice(2 * L * k, 2 * L * (k + 1))
            probs = pt[keys, columns]
            grad_probs = dot(vn[keys, :], grads_t)
            grad_scores = (probs.astype(f32) * (grad_probs - shift)).astype(bf16)
            grad_query += dot(qkt[2 * E - EP :, keys], grad_scores)
            dv_sum[keys, :] += dot(probs, grads_n)
            dk_sum[keys, :] += dot(grad_scores, queries)
        dq_send[:, columns] = rows_to(grad_query[EP - E :] * scaling, EP).astype(bf16)

    def first_core(i):
        quad = quad_at(i)
        first, second = members(0, quad)
        take_grads(first)
        take_grads(second)
        backward_queries(quad)
        unless_me(first, send_dq)
        unless_me(second, send_dq)

    each(1, quads, first_core)
    first_core(0 * me)

    def take_second(i):
        quad = quad_at(i)
        first, second = members(1, quad)
        take_grads(first)
        take_grads(second)

    each(0, quads, take_second)
    half = pairs * L

    def backward_keys(pair):
        rows = block(pair, 2 * L)
        probs = pt[rows, half:]
        grad_probs = dot(vn[rows, :], dot_t[:, half:])
        grad_scores = (probs.astype(f32) * (grad_probs - correction[:, half:])).astype(bf16)
        grad_value = dv_sum[rows, :] + dot(probs, dot_n[half:, :])
        grad_key = (dk_sum[rows, :] + dot(grad_scores, qn[half:, :])) * scaling
        dq[...] += dot(qkt[2 * E - EP :, rows], grad_scores)
        dkv_send[:, rows] = jnp.concatenate([grad_key.T[:E], grad_value.T[:E]]).astype(bf16)

    def second_core(i):
        quad = quad_at(i)
        for core in range(2):
            first, second = members(core, quad)
            backward_keys(core * quads + quad)
            unless_me(first, send_dkv)
            unless_me(second, send_dkv)

    each(1, quads, second_core)
    second_core(0 * me)
    dq_send[:, half:] = rows_to(dq[EP - E :, :] * scaling, EP).astype(bf16)

    def send_second(i):
        quad = quad_at(i)
        first, second = members(1, quad)
        unless_me(first, send_dq)
        unless_me(second, send_dq)

    send_second(0 * me)
    each(1, quads, send_second)
    own_dkv = pltpu.make_async_copy(dkv_send.at[:, place_of(me)], dkv_recv.at[me], local_sem.at[3])
    own_dkv.start()
    own_dq = pltpu.make_async_copy(dq_send.at[:, place_of(me)], dq_recv.at[me], local_sem.at[4])
    own_dq.start()

    each(1, nc, lambda j: clip_wait(PRED, pred_recv.at[clip_at(-j)], clip_at(-j)))
    for c in range(nc):
        prediction[c] = (pred_recv[c].astype(f32) * receiving[:, c : c + 1]).astype(bf16)

    def sent_clip(j):
        peer = clip_at(j)
        clip_copy(COT, cot_hbm.at[0, 0, peer], cot_recv.at[clip], peer).wait_send()
        clip_copy(PRED, pred_send, pred_recv.at[clip], peer).wait_send()

    def sent(j):
        peer = seq_at(j)
        seq_copy(QK, qk_send.at[peer], qkt.at[:, place_of(me)], peer).wait_send()
        seq_copy(V, v_send.at[peer], vt.at[:, place_of(me)], peer).wait_send()
        seq_copy(GRADS, grads_send.at[peer], dot_t.at[pl.ds(0, EP), place_of(me)], peer).wait_send()
        seq_copy(DKV, dkv_send.at[:, place_of(peer)], dkv_recv.at[me], peer).wait_send()
        seq_wait(DKV, dkv_recv.at[peer], peer)

    def last(j):
        peer = seq_at(j)
        seq_copy(DQ, dq_send.at[:, place_of(peer)], dq_recv.at[me], peer).wait_send()
        seq_wait(DQ, dq_recv.at[peer], peer)

    each(1, nc, sent_clip)
    own_dkv.wait()
    own_dq.wait()
    sent_core(1 + 3, quads, 0)
    sent_core(0, 1, 0)
    sent_core(0, quads, 1)
    each(1, ns, sent)
    each(1, ns, last)


def finish(ns, parts, masked, dkv, dq, prediction, qkv_grad, xt, turned, sems):
    tiles = qkv_grad.shape[2] // L
    thirds = tiles // 3
    each_part = masked.shape[0] // parts
    copies = []
    for p in range(parts):
        some = pl.ds(p * each_part, each_part)
        copies.append(pltpu.make_async_copy(masked.at[some], prediction.at[0, 0, some], sems.at[p]))
        copies[-1].start()
    for h in range(ns):
        first = 3 * E * h
        xt[first : first + E, :] = dq[h].astype(f32)[:E]
        xt[first + E : first + 3 * E, :] = dkv[h].astype(f32)
    for p in range(3):
        for j in range(p * thirds, (p + 1) * thirds):
            turned[:, j * L : (j + 1) * L] = xt[j * L : (j + 1) * L, :].T.astype(bf16)
        columns = pl.ds(p * thirds * L, thirds * L)
        copies.append(pltpu.make_async_copy(turned.at[:, columns], qkv_grad.at[0, :, columns], sems.at[parts + p]))
        copies[-1].start()
    for copy in copies:
        copy.wait()


def on_device(ns, nc, qkv, w_out, enc_gain, w_embed, pred_gain, ctx_blocks, owner, cotangent):
    d, width = w_embed.shape
    tokens = ns * L
    vmem = pl.BlockSpec(memory_space=pltpu.VMEM)
    hbm = pl.BlockSpec(memory_space=pl.ANY)
    scratch = [
        pltpu.VMEM((3 * d + 16, L), f32),
        pltpu.VMEM((L, 3 * d), bf16),
        pltpu.VMEM((d, d), bf16),
        pltpu.VMEM((d, width), bf16),
        pltpu.VMEM((ns, 2 * E, L), bf16),
        pltpu.VMEM((ns, EP, L), bf16),
        pltpu.VMEM((2 * E, tokens), bf16),
        pltpu.VMEM((EP, tokens), bf16),
        pltpu.VMEM((L, tokens), bf16),
        pltpu.VMEM((tokens, L), bf16),
        pltpu.VMEM((tokens, L), bf16),
        pltpu.VMEM((tokens, L), bf16),
        pltpu.VMEM((tokens, tokens), bf16),
        pltpu.VMEM((EP, tokens), bf16),
        pltpu.VMEM((tokens, 2 * L), f32),
        pltpu.VMEM((1, tokens), f32),
        pltpu.VMEM((1, tokens), f32),
        pltpu.VMEM((ns, EP, L), bf16),
        pltpu.VMEM((L, d), bf16),
        pltpu.VMEM((nc, L, width), bf16),
        pltpu.VMEM((L, width), bf16),
        pltpu.VMEM((nc, L, width), bf16),
        pltpu.VMEM((ns, EP, L), bf16),
        pltpu.VMEM((L, tokens), bf16),
        pltpu.VMEM((tokens, L), bf16),
        pltpu.VMEM((EP, tokens // 2), f32),
        pltpu.VMEM((tokens, L), f32),
        pltpu.VMEM((tokens, L), f32),
        pltpu.VMEM((2 * E, tokens), bf16),
        pltpu.VMEM((EP, tokens), bf16),
        pltpu.SemaphoreType.DMA((6, ns)),
        pltpu.SemaphoreType.DMA((6, ns)),
        pltpu.SemaphoreType.DMA((2, nc)),
        pltpu.SemaphoreType.DMA((2, nc)),
        pltpu.SemaphoreType.DMA((9,)),
        pltpu.SemaphoreType.REGULAR,
    ]
    prediction, dkv, dq = pl.pallas_call(
        functools.partial(kernel, ns, nc),
        out_shape=(
            pltpu.VMEM((nc, L, width), bf16),
            pltpu.VMEM((ns, 2 * E, L), bf16),
            pltpu.VMEM((ns, EP, L), bf16),
        ),
        in_specs=[hbm, hbm, vmem, hbm, vmem, vmem, vmem, hbm],
        out_specs=(vmem, vmem, vmem),
        scratch_shapes=scratch,
        compiler_params=pltpu.CompilerParams(
            collective_id=0, has_side_effects=True, vmem_limit_bytes=56 * 1024 * 1024
        ),
        cost_estimate=pl.CostEstimate(flops=16_000_000_000, bytes_accessed=12_000_000, transcendentals=4_194_304),
    )(qkv, w_out, enc_gain, w_embed, pred_gain, ctx_blocks.T, owner[None], cotangent)
    parts = min(nc, 4)
    return pl.pallas_call(
        functools.partial(finish, ns, parts),
        out_shape=(
            jax.ShapeDtypeStruct((1, 1, nc, L, width), bf16),
            jax.ShapeDtypeStruct((1, L, 3 * d), bf16),
        ),
        in_specs=[vmem, vmem, vmem],
        out_specs=(hbm, hbm),
        scratch_shapes=[
            pltpu.VMEM((3 * d, L), f32),
            pltpu.VMEM((L, 3 * d), bf16),
            pltpu.SemaphoreType.DMA((3 + parts,)),
        ],
        compiler_params=pltpu.CompilerParams(vmem_limit_bytes=14 * 1024 * 1024),
        cost_estimate=pl.CostEstimate(flops=0, bytes_accessed=6_000_000, transcendentals=0),
    )(prediction, dkv, dq)


def solution(mesh):
    placed = (
        P("clip", "seq", None),
        P(),
        P(),
        P(),
        P(),
        P(),
        P(),
        P("clip", "seq", None, None, None),
    )
    return jax.shard_map(
        functools.partial(on_device, mesh.shape["seq"], mesh.shape["clip"]),
        mesh=mesh,
        in_specs=placed,
        out_specs=(P("clip", "seq", None, None, None), P("clip", "seq", None)),
        check_vma=False,
    )
```
